32 devices in a mesh: group: 1, wide: 32 (over z, y, x, core).
Axes of the slice: x: 2, y: 2, z: 4, core: 2. Of those that a mesh axis runs over, the one named last changes fastest.
Arguments:
- resid: bfloat16 [32, 3072], P(('group', 'wide')), may hold values from -6 to 6
- query: bfloat16 [32, 4096], P(('group', 'wide')), may hold values from -4 to 4
- key: bfloat16 [32, 4096], P(('group', 'wide')), may hold values from -4 to 4
- value: bfloat16 [32, 4096], P(('group', 'wide')), may hold values from -6 to 6
- state: float32 [32, 32, 128, 128], P(('group', 'wide')), may hold values from -6 to 6
- decay: float32 [32], replicated, may hold values from 0.02 to 2
- out_gate: bfloat16 [32, 4096], P(('group', 'wide')), may hold values from -6 to 6
- norm_gain: float32 [4096], replicated, may hold values from 0.25 to 1.75
- w_out: bfloat16 [4096, 3072], P('wide'), may hold values from -0.09375 to 0.09375
- moe_gain: float32 [3072], replicated, may hold values from 0.25 to 1.75
- w_gate: bfloat16 [32, 576, 3072], P('wide'), may hold values from -0.109375 to 0.109375
- w_up: bfloat16 [32, 576, 3072], P('wide'), may hold values from -0.109375 to 0.109375
- w_down: bfloat16 [32, 576, 3072], P('wide'), may hold values from -0.09375 to 0.09375
- expert_ids: int32 [32, 2], P('group'), may hold values from 0 to 3, all different within a row; in each aligned block of 32 rows (0 to 31, 32 to 63, ...) at most 32 rows name the same one
- expert_weights: float32 [32, 2], P('group'), may hold values from 0.2 to 1
Outputs:
- mixed: bfloat16 [32, 3072], P(('group', 'wide'))
The draws below stay inside these ranges and needn't reach their ends.
Inputs may be any that keep to these rules, and one draw needn't show every extreme that they name: `expert_ids`: each request names two different experts; every expert is named by some request; no expert is named by more than 32 requests, a bound that some block reaches.
All inputs are finite; a program needn't handle non-finite values.
Results may differ from the reference program's by a relative error of at most 0.012.
Values may be sent and summed in bfloat16 or wider, within the bound.
A program may use at most 64 MiB of HBM per device.

```python
import math
import jax
import jax.numpy as jnp
import numpy as np
from jax import lax

D = 3072
HEADS = 32
HDIM = 128
FF = 4608
SPLIT = 8
ROWS = 32
EXPERTS = 4
CAP = 32
FF_DEV = 576
ATT = 4096


def block_scale(key, shape, pieces, smallest, top_value):
    def one(axis_at, shards_of):
        heights = jax.random.uniform(jax.random.fold_in(jax.random.fold_in(key, 6), axis_at), (shards_of,), jnp.float32, smallest / len(pieces), top_value / len(pieces))
        return jnp.repeat(jnp.exp(heights), shape[axis_at] // shards_of).reshape((-1,) + (1,) * (len(shape) - axis_at - 1))

    level = one(*pieces[0])
    for cut in pieces[1:]:
        level = level * one(*cut)
    return level


def assign_block(rng, own, number, rows, amount, top, reach, skew):
    order = jax.random.permutation(rng, amount)
    packed, common = shares(amount, rows * top, reach, skew, True), shares(amount, rows * top, reach, skew, False)
    places = jnp.arange(amount)

    def named(lengths, turn):
        used = int((lengths > 0).sum())
        fixed = max(1, used // 4)
        moved = fixed + (places - fixed + turn * (used - fixed)) % max(1, amount - fixed)
        return jnp.zeros((amount,), jnp.int32).at[order[jnp.where(places < fixed, places, moved)]].set(jnp.asarray(lengths, jnp.int32))

    lengths = jnp.where(number % 4 == 0, named(packed, number // 4), named(common, number - number // 4 - 1))
    mixed = jax.random.permutation(jax.random.fold_in(own, 3), amount)
    donor, taker = mixed[0:amount // 2 * 2:2], mixed[1:amount // 2 * 2:2]
    margin = jnp.minimum(lengths[donor] - 1, reach - lengths[taker]) // 2
    margin = jnp.where((donor == order[0]) | (taker == order[0]) | (lengths[taker] == 0), 0, jnp.maximum(margin, 0))
    moved = jax.random.randint(jax.random.fold_in(own, 4), (amount // 2,), 0, 1 << 20) % (margin + 1)
    lengths = lengths.at[donor].add(-moved).at[taker].add(moved)
    items = jnp.searchsorted(jnp.cumsum(lengths), jnp.arange(rows * top), side="right").astype(jnp.int32)
    table = items.reshape(top, rows).T
    table = table[jax.random.permutation(jax.random.fold_in(own, 1), rows)]
    turn = jax.random.randint(jax.random.fold_in(own, 2), (rows, 1), 0, top)
    return jnp.take_along_axis(table, (jnp.arange(top)[None, :] + turn) % top, axis=1)


def shares(amount, total, limit, lean, full):
    weights = [(1 << 20) // math.isqrt(grade ** lean) + 1 for grade in range(1, amount + 1)]
    largest = limit if full else min(limit, max(-(-total // amount), total * weights[0] // sum(weights)))
    least = 1 if total - largest >= amount - 1 else 0
    holding, spare = [largest] + [least] * (amount - 1), total - largest - least * (amount - 1)
    while spare > 0:
        candidates = [i for i in range(1, amount) if holding[i] < largest] or [i for i in range(1, amount) if holding[i] < limit]
        mass, left = sum([weights[i] for i in candidates]), spare
        for i in candidates:
            more = min(limit - holding[i], max(1, left * weights[i] // mass), spare)
            holding[i] = holding[i] + more
            spare = spare - more
    return np.array(holding)


def noise(own_key, extent, scale, reach, shards=(), held_as=jnp.bfloat16):
    entries = scale * jax.random.normal(own_key, extent, jnp.float32)
    if shards:
        entries = entries * block_scale(own_key, extent, shards, -0.22, 0.18)
    return jnp.clip(entries, -reach, reach).astype(held_as)


def setup_inputs(seed: int = 0, part: int = 0) -> dict:
    seeds = jax.random.split(jax.random.key(seed), 16)
    part_splits = jax.random.split(jax.random.fold_in(seeds[15], part), 16)
    resid = noise(part_splits[0], (ROWS, D), 1.0, 6.0, ((0, 32),))
    query = noise(part_splits[1], (ROWS, ATT), 0.3, 4.0, ((0, 32),))
    key = noise(part_splits[2], (ROWS, ATT), 0.3, 4.0, ((0, 32),))
    value = noise(part_splits[3], (ROWS, ATT), 1.0, 6.0, ((0, 32),))
    state = noise(part_splits[4], (ROWS, HEADS, HDIM, HDIM), 0.5, 6.0, ((0, 32),), jnp.float32)
    decay = jnp.clip(jnp.exp(jax.random.uniform(seeds[5], (HEADS,), jnp.float32, math.log(0.02), math.log(2.0))), 0.02, 2.0)
    out_gate = noise(part_splits[6], (ROWS, ATT), 1.0, 6.0, ((0, 32),))
    norm_gain = jnp.clip(1.0 + 0.15 * jax.random.normal(seeds[7], (ATT,), jnp.float32), 0.25, 1.75)
    w_out = noise(seeds[8], (ATT, D), ATT ** -0.5, 0.09375, ((0, 32),))
    moe_gain = jnp.clip(1.0 + 0.15 * jax.random.normal(seeds[9], (D,), jnp.float32), 0.25, 1.75)
    w_gate = noise(seeds[10], (EXPERTS * SPLIT, FF_DEV, D), D ** -0.5, 0.109375, ((0, 32),))
    w_up = noise(seeds[11], (EXPERTS * SPLIT, FF_DEV, D), D ** -0.5, 0.109375, ((0, 32),))
    w_down = noise(seeds[12], (EXPERTS * SPLIT, FF_DEV, D), FF ** -0.5, 0.09375, ((0, 32),))
    expert_ids_keys = jax.random.split(jax.random.fold_in(part_splits[13], 1), ROWS // ROWS)
    expert_ids_turns = jax.random.permutation(jax.random.fold_in(part_splits[13], 3), ROWS // ROWS)
    expert_ids = jax.vmap(lambda own, number: assign_block(jax.random.fold_in(part_splits[13], 2), own, number, ROWS, EXPERTS, 2, CAP, 2))(expert_ids_keys, expert_ids_turns).reshape((ROWS, 2))
    expert_weights = jnp.clip(jax.random.uniform(part_splits[14], (ROWS, 2), jnp.float32, 0.2, 1.0), 0.2, 1.0)
    return {"resid": resid, "query": query, "key": key, "value": value, "state": state, "decay": decay, "out_gate": out_gate, "norm_gain": norm_gain, "w_out": w_out, "moe_gain": moe_gain, "w_gate": w_gate, "w_up": w_up, "w_down": w_down, "expert_ids": expert_ids, "expert_weights": expert_weights}


def by_rows(left, weight):
    return lax.dot_general(left, weight, (((1,), (1,)), ((), ())), preferred_element_type=jnp.float32)

def reference(resid, query, key, value, state, decay, out_gate, norm_gain, w_out, moe_gain, w_gate, w_up, w_down, expert_ids, expert_weights):
    rows = resid.shape[0]
    q_heads = query.astype(jnp.float32).reshape(rows, HEADS, HDIM)
    k_heads = key.astype(jnp.float32).reshape(rows, HEADS, HDIM)
    v_heads = value.astype(jnp.float32).reshape(rows, HEADS, HDIM)
    fade = jnp.exp(-decay)
    new_state = fade[None, :, None, None] * state + jnp.einsum('rhi,rhj->rhij', k_heads, v_heads)
    att = jnp.einsum('rhi,rhij->rhj', q_heads, new_state).reshape(rows, HEADS * HDIM)
    scale = lax.rsqrt(lax.optimization_barrier(jnp.mean(att * att, axis=1, keepdims=True)) + 1e-06)
    attn = (att * scale * norm_gain * jax.nn.sigmoid(out_gate.astype(jnp.float32))).astype(jnp.bfloat16)
    proj = jnp.dot(attn, w_out, preferred_element_type=jnp.float32)
    hid_res = (resid.astype(jnp.float32) + proj).astype(jnp.bfloat16)
    hid_f = hid_res.astype(jnp.float32)
    normed = (hid_f * lax.rsqrt(lax.optimization_barrier(jnp.mean(hid_f * hid_f, axis=1, keepdims=True)) + 1e-06) * moe_gain).astype(jnp.bfloat16)
    experts = jnp.arange(EXPERTS, dtype=jnp.int32)
    coef = lax.optimization_barrier(jnp.sum(jnp.where(expert_ids[:, :, None] == experts[None, None, :], expert_weights[:, :, None], 0.0), axis=1))
    slabs = jnp.arange(EXPERTS * SPLIT, dtype=jnp.int32)

    def one_slab(total, inputs):
        gate_w, up_w, down_w, slab = inputs
        gate = by_rows(normed, gate_w)
        upper = by_rows(normed, up_w)
        inner = (jax.nn.silu(gate) * upper).astype(jnp.bfloat16)
        weight = lax.optimization_barrier(jnp.sum(jnp.where(experts[None, :] == slab // SPLIT, coef, 0.0), axis=1))
        part = jnp.dot(inner, down_w, preferred_element_type=jnp.float32) * weight[:, None]
        return (total + part, None)
    total, _ = lax.scan(one_slab, jnp.zeros((rows, D), jnp.float32), (w_gate, w_up, w_down, slabs))
    return (hid_f + total).astype(jnp.bfloat16)
```

```python
import functools

import jax
import jax.numpy as jnp
from jax import lax
from jax.experimental import pallas as pl
from jax.experimental.pallas import tpu as pltpu
from jax.sharding import PartitionSpec as P

F32, BF16 = jnp.float32, jnp.bfloat16
TILE = 16
STATE_CUTS = 4
VMEM = 44 * 1024 * 1024


def iota(shape, dim):
    return lax.broadcasted_iota(jnp.int32, shape, dim)


def dot(left, right):
    return jnp.dot(left, right, preferred_element_type=F32)


def by_rows(left, weight):
    return lax.dot_general(left, weight, (((1,), (1,)), ((), ())), preferred_element_type=F32)


def layout(n, width):
    inner = 1
    while inner * inner < n:
        inner *= 2
    outer = n // inner
    pieces = max(1, TILE // outer)
    columns = width // pieces
    chunks = max(c for c in (1, 2, 3, 4) if (columns // 128) % c == 0)
    return inner, outer, pieces, columns, chunks


def kernel(
    n, slab_split,
    resid, query, key, value, decay, out_gate, norm_gain, moe_gain, ids, weights,
    state_h, w_out_h, w_gate_h, w_up_h, w_down_h,
    out,
    state, w_out, w_gate, w_up, w_down,
    heads5, rows2, att3, recv1, send_a, recv_a, send_b, recv_b, recv_c, recv_d,
    xs, send_e, recv_e, send_f, recv_f,
    load_sem, send_sem, recv_sem, chunk_send, chunk_recv, last_send, last_recv,
):
    heads, hdim = att3.shape[0], att3.shape[2]
    width = resid.shape[1]
    inner, outer, pieces, columns, chunks = layout(n, width)
    step = columns // chunks
    share = w_out_h.shape[0]
    me = lax.axis_index("wide")
    a, b = me // inner, me % inner
    tile = outer * pieces

    barrier = pltpu.get_barrier_semaphore()

    def greet(i, carry):
        pl.semaphore_signal(
            barrier, inc=1, device_id={"wide": (me + i) % n},
            device_id_type=pl.DeviceIdType.MESH,
        )
        return carry

    part = state.shape[0] // STATE_CUTS
    loads = []
    for c in range(STATE_CUTS):
        at = pl.ds(c * part, part)
        loads.append(pltpu.make_async_copy(state_h.at[at], state.at[at], load_sem.at[c]))
        loads[-1].start()
    if share == hdim:
        get_out = pltpu.make_async_copy(w_out_h, w_out, load_sem.at[STATE_CUTS])
    else:
        w_out[...] = jnp.zeros_like(w_out)
        place = pl.ds(pl.multiple_of((me * share) % hdim, share), share)
        get_out = pltpu.make_async_copy(w_out_h, w_out.at[place], load_sem.at[STATE_CUTS])
    get_out.start()
    big = []
    for i, (src, dst) in enumerate(((w_gate_h, w_gate), (w_up_h, w_up), (w_down_h, w_down))):
        big.append(pltpu.make_async_copy(src.at[0], dst, load_sem.at[STATE_CUTS + 1 + i]))
        big[-1].start()

    lax.fori_loop(1, n, greet, 0)

    for i, ref in enumerate((query, key, value, out_gate, norm_gain)):
        line = ref[...].astype(F32)
        for h in range(heads):
            heads5[i, h : h + 1, :] = line[:, h * hdim : (h + 1) * hdim]
    for i, ref in enumerate((resid, moe_gain)):
        line = ref[...].astype(F32)
        for p in range(pieces):
            rows2[i, p : p + 1, :] = line[:, p * columns : (p + 1) * columns]
    q, k, v = heads5[0], heads5[1], heads5[2]
    head_of = iota((heads, hdim), 0)
    eye = iota((heads, heads), 0) == iota((heads, heads), 1)
    fade = jnp.sum(
        jnp.where(eye, jnp.broadcast_to(jnp.exp(-decay[...]), (heads, heads)), 0.0),
        axis=1, keepdims=True,
    )
    att = jnp.zeros((heads, hdim), F32)
    per_cut = heads // STATE_CUTS
    for c in range(STATE_CUTS):
        diagonal = jnp.concatenate(
            [jnp.where(head_of == c * per_cut + h, q, 0.0).astype(BF16) for h in range(per_cut)],
            axis=1,
        )
        loads[c].wait()
        att += dot(diagonal, state[pl.ds(c * part, part), :].astype(BF16))
    att = fade * att + jnp.sum(q * k, axis=1, keepdims=True) * v
    mean = jnp.sum(jnp.sum(att * att, axis=1, keepdims=True), axis=0, keepdims=True) / (
        heads * hdim
    )
    attn = att * lax.rsqrt(mean + 1e-06) * heads5[4] * jax.nn.sigmoid(heads5[3])
    att3[...] = attn.reshape(heads, 1, hdim)

    pl.semaphore_wait(barrier, n - 1)

    slot = b * outer + a

    def send_head(i, carry):
        peer = (me + i) % n
        pltpu.make_async_remote_copy(
            src_ref=att3.at[(peer * share) // hdim], dst_ref=recv1.at[slot],
            send_sem=send_sem.at[0], recv_sem=recv_sem.at[0],
            device_id={"wide": peer}, device_id_type=pl.DeviceIdType.MESH,
        ).start()
        return carry

    lax.fori_loop(1, n, send_head, 0)
    recv1[slot] = att3[(me * share) // hdim]

    def settle(ref, count, sem):
        view = ref.at[pl.ds(0, count)]
        pltpu.make_async_copy(view, view, sem).wait()

    def to_inner(src, dst, ssem, rsem, pick):
        def one(i, carry):
            peer = (b + i) % inner
            pltpu.make_async_remote_copy(
                src_ref=src.at[peer if pick else b], dst_ref=dst.at[b],
                send_sem=ssem, recv_sem=rsem,
                device_id={"wide": a * inner + peer}, device_id_type=pl.DeviceIdType.MESH,
            ).start()
            return carry

        lax.fori_loop(1, inner, one, 0)

    def to_outer(src, dst, ssem, rsem, pick):
        def one(i, carry):
            peer = (a + i) % outer
            pltpu.make_async_remote_copy(
                src_ref=src.at[peer if pick else a], dst_ref=dst.at[a],
                send_sem=ssem, recv_sem=rsem,
                device_id={"wide": peer * inner + b}, device_id_type=pl.DeviceIdType.MESH,
            ).start()
            return carry

        lax.fori_loop(1, outer, one, 0)

    lines = n * pieces
    spread = (iota((lines, n), 0) // pieces == iota((lines, n), 1)).astype(F32).astype(BF16)
    piece_of = iota((lines, 1), 0) % pieces

    def only(p, full):
        return jnp.where(piece_of == p, full, 0.0).astype(BF16)

    owner = me // slab_split
    coef = jnp.sum(jnp.where(ids[...] == owner, weights[...], 0.0), axis=1, keepdims=True)
    line = iota((n, lines), 1) // pieces
    request = (line % outer) * inner + line // outer
    coef_row = jnp.sum(
        jnp.where(request == iota((n, lines), 0), jnp.broadcast_to(coef, (n, lines)), 0.0),
        axis=0, keepdims=True,
    )
    same = iota((lines, lines), 0) == iota((lines, lines), 1)
    coef_line = jnp.sum(
        jnp.where(same, jnp.broadcast_to(coef_row, (lines, lines)), 0.0), axis=1, keepdims=True
    )

    get_out.wait()
    settle(recv1, n - 1, recv_sem.at[0])
    full = dot(spread, recv1[...].reshape(n, hdim).astype(BF16))
    proj = jnp.zeros((lines, columns), F32)
    for p in range(pieces):
        proj += dot(only(p, full), w_out[:, p * columns : (p + 1) * columns])
    send_a[...] = proj.astype(BF16).reshape(inner, tile, columns)
    to_inner(send_a, recv_a, send_sem.at[1], recv_sem.at[1], True)
    recv_a[b] = send_a[b]
    settle(recv_a, inner - 1, recv_sem.at[1])
    total = recv_a[0].astype(F32)
    for i in range(1, inner):
        total += recv_a[i].astype(F32)
    send_b[...] = total.reshape(outer, pieces, columns)
    to_outer(send_b, recv_b, send_sem.at[2], recv_sem.at[2], True)
    recv_b[a] = send_b[a]
    settle(recv_b, outer - 1, recv_sem.at[2])
    hid = (rows2[0] + jnp.sum(recv_b[...], axis=0)).astype(BF16).astype(F32)
    mean = jnp.sum(jnp.sum(hid * hid, axis=1, keepdims=True), axis=0, keepdims=True) / width
    recv_c[a] = hid * lax.rsqrt(mean + 1e-06) * rows2[1]

    to_outer(recv_c, recv_c, send_sem.at[3], recv_sem.at[3], False)
    settle(recv_c, outer - 1, recv_sem.at[3])
    recv_d[b] = recv_c[...].reshape(tile, columns).astype(BF16)
    to_inner(recv_d, recv_d, send_sem.at[4], recv_sem.at[4], False)
    settle(recv_d, inner - 1, recv_sem.at[4])
    normed = recv_d[...].reshape(lines, columns)
    at_line = iota((n, lines), 0) * pieces
    for p in range(pieces):
        pick = (iota((n, lines), 1) == at_line + p).astype(F32).astype(BF16)
        xs[p] = dot(pick, normed).astype(BF16)

    big[0].wait()
    big[1].wait()
    hidden = w_gate.shape[0]

    def piece(p, carry):
        gate, upper = carry
        at = pl.ds(pl.multiple_of(p * columns, columns), columns)
        x = xs[p]
        return gate + by_rows(x, w_gate[:, at]), upper + by_rows(x, w_up[:, at])

    zero = jnp.zeros((n, hidden), F32)
    gate, upper = lax.fori_loop(0, pieces, piece, (zero, zero))
    inner_act = (gate * jax.nn.sigmoid(gate) * upper).astype(BF16)
    full = dot(spread, inner_act)
    big[2].wait()
    for j in range(chunks):
        acc = jnp.zeros((lines, step), F32)
        for p in range(pieces):
            start = p * columns + j * step
            acc += dot(only(p, full), w_down[:, start : start + step])
        send_e[j] = (acc * coef_line).astype(BF16).reshape(inner, tile, step)
        to_inner(send_e.at[j], recv_e.at[j], chunk_send.at[j], chunk_recv.at[j], True)
        recv_e[j, b] = send_e[j, b]
    for j in range(chunks):
        settle(recv_e.at[j], inner - 1, chunk_recv.at[j])
        total = recv_e[j, 0].astype(F32)
        for i in range(1, inner):
            total += recv_e[j, i].astype(F32)
        send_f[j] = total.reshape(outer, pieces, step)
        to_outer(send_f.at[j], recv_f.at[j], last_send.at[j], last_recv.at[j], True)
        recv_f[j, a] = send_f[j, a]
    for j in range(chunks):
        settle(recv_f.at[j], outer - 1, last_recv.at[j])
        mixed = (hid[:, j * step : (j + 1) * step] + jnp.sum(recv_f[j], axis=0)).astype(BF16)
        for p in range(pieces):
            start = p * columns + j * step
            out[:, start : start + step] = mixed[p : p + 1, :]

    settle(recv1, n - 1, send_sem.at[0])
    settle(send_a, inner - 1, send_sem.at[1])
    settle(send_b, outer - 1, send_sem.at[2])
    settle(recv_c, outer - 1, send_sem.at[3])
    settle(recv_d, inner - 1, send_sem.at[4])
    for j in range(chunks):
        settle(send_e.at[j], inner - 1, chunk_send.at[j])
        settle(send_f.at[j], outer - 1, last_send.at[j])


def shards(
    resid, query, key, value, state, decay, out_gate, norm_gain, w_out, moe_gain,
    w_gate, w_up, w_down, expert_ids, expert_weights, *, slab_split,
):
    n = lax.axis_size("wide")
    width = resid.shape[1]
    heads, hdim = state.shape[1], state.shape[2]
    inner, outer, pieces, columns, chunks = layout(n, width)
    step = columns // chunks
    tile = outer * pieces
    hidden = w_gate.shape[1]
    vmem = pl.BlockSpec(memory_space=pltpu.VMEM)
    hbm = pl.BlockSpec(memory_space=pl.ANY)
    sems = pltpu.SemaphoreType.DMA
    return pl.pallas_call(
        functools.partial(kernel, n, slab_split),
        out_shape=jax.ShapeDtypeStruct(resid.shape, resid.dtype),
        in_specs=[vmem] * 10 + [hbm] * 5,
        out_specs=vmem,
        scratch_shapes=[
            pltpu.VMEM((heads * hdim, hdim), F32),
            pltpu.VMEM((hdim, width), BF16),
            pltpu.VMEM((hidden, width), BF16),
            pltpu.VMEM((hidden, width), BF16),
            pltpu.VMEM((hidden, width), BF16),
            pltpu.VMEM((5, heads, hdim), F32),
            pltpu.VMEM((2, pieces, columns), F32),
            pltpu.VMEM((heads, 1, hdim), F32),
            pltpu.VMEM((n, 1, hdim), F32),
            pltpu.VMEM((inner, tile, columns), BF16),
            pltpu.VMEM((inner, tile, columns), BF16),
            pltpu.VMEM((outer, pieces, columns), F32),
            pltpu.VMEM((outer, pieces, columns), F32),
            pltpu.VMEM((outer, pieces, columns), F32),
            pltpu.VMEM((inner, tile, columns), BF16),
            pltpu.VMEM((pieces, n, columns), BF16),
            pltpu.VMEM((chunks, inner, tile, step), BF16),
            pltpu.VMEM((chunks, inner, tile, step), BF16),
            pltpu.VMEM((chunks, outer, pieces, step), F32),
            pltpu.VMEM((chunks, outer, pieces, step), F32),
            sems((STATE_CUTS + 4,)),
            sems((5,)),
            sems((5,)),
            sems((chunks,)),
            sems((chunks,)),
            sems((chunks,)),
            sems((chunks,)),
        ],
        compiler_params=pltpu.CompilerParams(
            collective_id=0, has_side_effects=True, vmem_limit_bytes=VMEM
        ),
        name="decode_layer",
    )(
        resid, query, key, value, decay.reshape(1, -1), out_gate, norm_gain.reshape(1, -1),
        moe_gain.reshape(1, -1), expert_ids, expert_weights,
        state.reshape(heads * hdim, hdim), w_out, w_gate, w_up, w_down,
    )


SPLIT = 8


def solution(mesh):
    rows = P(("group", "wide"), None)
    return jax.shard_map(
        functools.partial(shards, slab_split=SPLIT),
        mesh=mesh,
        in_specs=(
            rows, rows, rows, rows,
            P(("group", "wide"), None, None, None),
            P(), rows, P(), P("wide", None), P(),
            P("wide", None, None), P("wide", None, None), P("wide", None, None),
            P("group", None), P("group", None),
        ),
        out_specs=rows,
        check_vma=False,
    )
```

```python
import functools

import jax
import jax.numpy as jnp
from jax import lax
from jax.experimental import pallas as pl
from jax.experimental.pallas import tpu as pltpu
from jax.sharding import PartitionSpec as P

F32, BF16 = jnp.float32, jnp.bfloat16
TILE = 16
STATE_CUTS = 4
VMEM = 63 * 1024 * 1024


def iota(shape, dim):
    return lax.broadcasted_iota(jnp.int32, shape, dim)


def dot(left, right):
    return jnp.dot(left, right, preferred_element_type=F32)


def by_rows(left, weight):
    return lax.dot_general(left, weight, (((1,), (1,)), ((), ())), preferred_element_type=F32)


def layout(n, width):
    inner = 1
    while inner * inner < n:
        inner *= 2
    outer = n // inner
    pieces = max(1, TILE // outer)
    columns = width // pieces
    chunks = max(c for c in (1, 2, 3, 4) if (columns // 128) % c == 0)
    return inner, outer, pieces, columns, chunks


def kernel(
    n, slab_split,
    resid_h, query_h, key_h, value_h, decay_h, out_gate_h, norm_gain_h, moe_gain_h, ids_h, weights_h,
    state_h, w_out_h, w_gate_h, w_up_h, w_down_h,
    out,
    resid, query, key, value, decay, out_gate, norm_gain, moe_gain, ids, weights,
    state, w_out, w_gate, w_up, w_down,
    heads5, gains, hids, att3, recv1, send_a, recv_a, recv_r, recv_b, recv_d,
    xs, send_e, recv_e, send_f, recv_f,
    small_sem, load_sem, send_sem, recv_sem, chunk_send, chunk_recv, last_send, last_recv,
):
    heads, hdim = att3.shape[0], att3.shape[2]
    width = resid.shape[1]
    inner, outer, pieces, columns, chunks = layout(n, width)
    step = columns // chunks
    share = w_out_h.shape[0]
    me = lax.axis_index("wide")
    a, b = me // inner, me % inner
    tile = outer * pieces

    barrier = pltpu.get_barrier_semaphore()

    def greet(i, carry):
        pl.semaphore_signal(
            barrier, inc=1, device_id={"wide": (me + i) % n},
            device_id_type=pl.DeviceIdType.MESH,
        )
        return carry

    small = []
    for i, (src, dst) in enumerate((
        (query_h, query), (key_h, key), (value_h, value), (out_gate_h, out_gate),
        (norm_gain_h, norm_gain), (decay_h, decay), (resid_h, resid),
        (moe_gain_h, moe_gain), (ids_h, ids), (weights_h, weights),
    )):
        small.append(pltpu.make_async_copy(src, dst, small_sem.at[i]))
        small[-1].start()
    part = state.shape[0] // STATE_CUTS
    loads = []
    for c in range(STATE_CUTS):
        at = pl.ds(c * part, part)
        loads.append(pltpu.make_async_copy(state_h.at[at], state.at[at], load_sem.at[c]))
        loads[-1].start()
    if share == hdim:
        get_out = pltpu.make_async_copy(w_out_h, w_out, load_sem.at[STATE_CUTS])
    else:
        w_out[...] = jnp.zeros_like(w_out)
        place = pl.ds(pl.multiple_of((me * share) % hdim, share), share)
        get_out = pltpu.make_async_copy(w_out_h, w_out.at[place], load_sem.at[STATE_CUTS])
    get_out.start()
    big = []
    for i, (src, dst) in enumerate(((w_gate_h, w_gate), (w_up_h, w_up), (w_down_h, w_down))):
        big.append(pltpu.make_async_copy(src.at[0], dst, load_sem.at[STATE_CUTS + 1 + i]))
        big[-1].start()

    lax.fori_loop(1, n, greet, 0)

    for copy in small:
        copy.wait()
    for i, ref in enumerate((query, key, value, out_gate, norm_gain)):
        line = ref[...].astype(F32)
        for h in range(heads):
            heads5[i, h : h + 1, :] = line[:, h * hdim : (h + 1) * hdim]
    line = resid[...].astype(F32)
    for p in range(pieces):
        recv_r[a, p : p + 1, :] = line[:, p * columns : (p + 1) * columns]
        for i in range(outer):
            at = i * pieces + p
            gains[at : at + 1, :] = moe_gain[:, p * columns : (p + 1) * columns]
    q, k, v = heads5[0], heads5[1], heads5[2]
    head_of = iota((heads, hdim), 0)
    eye = iota((heads, heads), 0) == iota((heads, heads), 1)
    fade = jnp.sum(
        jnp.where(eye, jnp.broadcast_to(jnp.exp(-decay[...]), (heads, heads)), 0.0),
        axis=1, keepdims=True,
    )
    att = jnp.zeros((heads, hdim), F32)
    per_cut = heads // STATE_CUTS
    for c in range(STATE_CUTS):
        diagonal = jnp.concatenate(
            [jnp.where(head_of == c * per_cut + h, q, 0.0).astype(BF16) for h in range(per_cut)],
            axis=1,
        )
        loads[c].wait()
        att += dot(diagonal, state[pl.ds(c * part, part), :].astype(BF16))
    att = fade * att + jnp.sum(q * k, axis=1, keepdims=True) * v
    mean = jnp.sum(jnp.sum(att * att, axis=1, keepdims=True), axis=0, keepdims=True) / (
        heads * hdim
    )
    attn = att * lax.rsqrt(mean + 1e-06) * heads5[4] * jax.nn.sigmoid(heads5[3])
    att3[...] = attn.reshape(heads, 1, hdim)

    pl.semaphore_wait(barrier, n - 1)

    slot = b * outer + a

    def send_head(i, carry):
        peer = (me + i) % n
        pltpu.make_async_remote_copy(
            src_ref=att3.at[(peer * share) // hdim], dst_ref=recv1.at[slot],
            send_sem=send_sem.at[0], recv_sem=recv_sem.at[0],
            device_id={"wide": peer}, device_id_type=pl.DeviceIdType.MESH,
        ).start()
        return carry

    lax.fori_loop(1, n, send_head, 0)
    recv1[slot] = att3[(me * share) // hdim]

    def settle(ref, count, sem):
        view = ref.at[pl.ds(0, count)]
        pltpu.make_async_copy(view, view, sem).wait()

    def to_inner(src, dst, ssem, rsem, pick):
        def one(i, carry):
            peer = (b + i) % inner
            pltpu.make_async_remote_copy(
                src_ref=src.at[peer if pick else b], dst_ref=dst.at[b],
                send_sem=ssem, recv_sem=rsem,
                device_id={"wide": a * inner + peer}, device_id_type=pl.DeviceIdType.MESH,
            ).start()
            return carry

        lax.fori_loop(1, inner, one, 0)

    def to_outer(src, dst, ssem, rsem, pick):
        def one(i, carry):
            peer = (a + i) % outer
            pltpu.make_async_remote_copy(
                src_ref=src.at[peer if pick else a], dst_ref=dst.at[a],
                send_sem=ssem, recv_sem=rsem,
                device_id={"wide": peer * inner + b}, device_id_type=pl.DeviceIdType.MESH,
            ).start()
            return carry

        lax.fori_loop(1, outer, one, 0)

    lines = n * pieces
    spread = (iota((lines, n), 0) // pieces == iota((lines, n), 1)).astype(F32).astype(BF16)
    piece_of = iota((lines, 1), 0) % pieces

    def only(p, full):
        return jnp.where(piece_of == p, full, 0.0).astype(BF16)

    owner = me // slab_split
    coef = jnp.sum(jnp.where(ids[...] == owner, weights[...], 0.0), axis=0, keepdims=True)
    line = iota((lines, n), 0) // pieces
    request = (line % outer) * inner + line // outer
    coef_line = jnp.sum(
        jnp.where(request == iota((lines, n), 1), jnp.broadcast_to(coef, (lines, n)), 0.0),
        axis=1, keepdims=True,
    )

    to_outer(recv_r, recv_r, send_sem.at[3], recv_sem.at[3], False)

    get_out.wait()
    settle(recv1, n - 1, recv_sem.at[0])
    full = dot(spread, recv1[...].reshape(n, hdim).astype(BF16))
    proj = jnp.zeros((lines, columns), F32)
    for p in range(pieces):
        proj += dot(only(p, full), w_out[:, p * columns : (p + 1) * columns])
    send_a[...] = proj.astype(BF16).reshape(inner, tile, columns)
    to_inner(send_a, recv_a, send_sem.at[1], recv_sem.at[1], True)
    recv_a[b] = send_a[b]
    settle(recv_a, inner - 1, recv_sem.at[1])
    total = recv_a[0].astype(F32)
    for i in range(1, inner):
        total += recv_a[i].astype(F32)
    recv_b[a] = total.astype(BF16)
    to_outer(recv_b, recv_b, send_sem.at[2], recv_sem.at[2], False)
    settle(recv_r, outer - 1, recv_sem.at[3])
    settle(recv_b, outer - 1, recv_sem.at[2])
    total = recv_b[0].astype(F32)
    for i in range(1, outer):
        total += recv_b[i].astype(F32)
    hid = (recv_r[...].reshape(tile, columns) + total).astype(BF16).astype(F32)
    hids[...] = hid.reshape(outer, pieces, columns)
    squares = jnp.sum(hid * hid, axis=1, keepdims=True)
    mates = iota((tile, tile), 0) // pieces == iota((tile, tile), 1) // pieces
    mean = jnp.sum(
        jnp.where(mates, jnp.broadcast_to(squares, (tile, tile)), 0.0), axis=0, keepdims=True
    ) / width
    mean = jnp.sum(
        jnp.where(iota((tile, tile), 0) == iota((tile, tile), 1), jnp.broadcast_to(mean, (tile, tile)), 0.0),
        axis=1, keepdims=True,
    )

    recv_d[b] = (hid * lax.rsqrt(mean + 1e-06) * gains[...]).astype(BF16)
    to_inner(recv_d, recv_d, send_sem.at[4], recv_sem.at[4], False)
    settle(recv_d, inner - 1, recv_sem.at[4])
    normed = recv_d[...].reshape(lines, columns)
    at_line = iota((n, lines), 0) * pieces
    for p in range(pieces):
        pick = (iota((n, lines), 1) == at_line + p).astype(F32).astype(BF16)
        xs[p] = dot(pick, normed).astype(BF16)

    big[0].wait()
    big[1].wait()
    hidden = w_gate.shape[0]

    def piece(p, carry):
        gate, upper = carry
        at = pl.ds(pl.multiple_of(p * columns, columns), columns)
        x = xs[p]
        return gate + by_rows(x, w_gate[:, at]), upper + by_rows(x, w_up[:, at])

    zero = jnp.zeros((n, hidden), F32)
    gate, upper = lax.fori_loop(0, pieces, piece, (zero, zero))
    inner_act = (gate * jax.nn.sigmoid(gate) * upper).astype(BF16)
    full = dot(spread, inner_act)
    big[2].wait()
    for j in range(chunks):
        acc = jnp.zeros((lines, step), F32)
        for p in range(pieces):
            start = p * columns + j * step
            acc += dot(only(p, full), w_down[:, start : start + step])
        send_e[j] = (acc * coef_line).astype(BF16).reshape(inner, tile, step)
        to_inner(send_e.at[j], recv_e.at[j], chunk_send.at[j], chunk_recv.at[j], True)
        recv_e[j, b] = send_e[j, b]
    for j in range(chunks):
        settle(recv_e.at[j], inner - 1, chunk_recv.at[j])
        total = recv_e[j, 0].astype(F32)
        for i in range(1, inner):
            total += recv_e[j, i].astype(F32)
        send_f[j] = total.reshape(outer, pieces, step)
        to_outer(send_f.at[j], recv_f.at[j], last_send.at[j], last_recv.at[j], True)
        recv_f[j, a] = send_f[j, a]
    own = hids[a]
    for j in range(chunks):
        settle(recv_f.at[j], outer - 1, last_recv.at[j])
        mixed = (own[:, j * step : (j + 1) * step] + jnp.sum(recv_f[j], axis=0)).astype(BF16)
        for p in range(pieces):
            start = p * columns + j * step
            out[:, start : start + step] = mixed[p : p + 1, :]

    settle(recv1, n - 1, send_sem.at[0])
    settle(send_a, inner - 1, send_sem.at[1])
    settle(recv_b, outer - 1, send_sem.at[2])
    settle(recv_r, outer - 1, send_sem.at[3])
    settle(recv_d, inner - 1, send_sem.at[4])
    for j in range(chunks):
        settle(send_e.at[j], inner - 1, chunk_send.at[j])
        settle(send_f.at[j], outer - 1, last_send.at[j])


def shards(
    resid, query, key, value, state, decay, out_gate, norm_gain, w_out, moe_gain,
    w_gate, w_up, w_down, expert_ids, expert_weights, *, slab_split,
):
    n = lax.axis_size("wide")
    width = resid.shape[1]
    heads, hdim = state.shape[1], state.shape[2]
    inner, outer, pieces, columns, chunks = layout(n, width)
    step = columns // chunks
    tile = outer * pieces
    hidden = w_gate.shape[1]
    hbm = pl.BlockSpec(memory_space=pltpu.HBM)
    small = (
        resid, query, key, value, decay.reshape(1, -1), out_gate, norm_gain.reshape(1, -1),
        moe_gain.reshape(1, -1), expert_ids.T, expert_weights.T,
    )
    sems = pltpu.SemaphoreType.DMA
    return pl.pallas_call(
        functools.partial(kernel, n, slab_split),
        out_shape=jax.ShapeDtypeStruct(resid.shape, resid.dtype),
        in_specs=[hbm] * 15,
        out_specs=pl.BlockSpec(memory_space=pltpu.VMEM),
        scratch_shapes=[pltpu.VMEM(x.shape, x.dtype) for x in small] + [
            pltpu.VMEM((heads * hdim, hdim), F32),
            pltpu.VMEM((hdim, width), BF16),
            pltpu.VMEM((hidden, width), BF16),
            pltpu.VMEM((hidden, width), BF16),
            pltpu.VMEM((hidden, width), BF16),
            pltpu.VMEM((5, heads, hdim), F32),
            pltpu.VMEM((tile, columns), F32),
            pltpu.VMEM((outer, pieces, columns), F32),
            pltpu.VMEM((heads, 1, hdim), F32),
            pltpu.VMEM((n, 1, hdim), F32),
            pltpu.VMEM((inner, tile, columns), BF16),
            pltpu.VMEM((inner, tile, columns), BF16),
            pltpu.VMEM((outer, pieces, columns), F32),
            pltpu.VMEM((outer, tile, columns), BF16),
            pltpu.VMEM((inner, tile, columns), BF16),
            pltpu.VMEM((pieces, n, columns), BF16),
            pltpu.VMEM((chunks, inner, tile, step), BF16),
            pltpu.VMEM((chunks, inner, tile, step), BF16),
            pltpu.VMEM((chunks, outer, pieces, step), F32),
            pltpu.VMEM((chunks, outer, pieces, step), F32),
            sems((10,)),
            sems((STATE_CUTS + 4,)),
            sems((5,)),
            sems((5,)),
            sems((chunks,)),
            sems((chunks,)),
            sems((chunks,)),
            sems((chunks,)),
        ],
        compiler_params=pltpu.CompilerParams(
            collective_id=0, has_side_effects=True, vmem_limit_bytes=VMEM
        ),
        name="decode_layer",
    )(
        *small,
        state.reshape(heads * hdim, hdim), w_out, w_gate, w_up, w_down,
    )


SPLIT = 8


def solution(mesh):
    rows = P(("group", "wide"), None)
    return jax.shard_map(
        functools.partial(shards, slab_split=SPLIT),
        mesh=mesh,
        in_specs=(
            rows, rows, rows, rows,
            P(("group", "wide"), None, None, None),
            P(), rows, P(), P("wide", None), P(),
            P("wide", None, None), P("wide", None, None), P("wide", None, None),
            P("group", None), P("group", None),
        ),
        out_specs=rows,
        check_vma=False,
    )
```

```python
import functools

import jax
import jax.numpy as jnp
from jax import lax
from jax.experimental import pallas as pl
from jax.experimental.pallas import tpu as pltpu
from jax.sharding import PartitionSpec as P

F32, BF16 = jnp.float32, jnp.bfloat16
TILE = 16
STATE_CUTS = 4
VMEM = 63 * 1024 * 1024


def iota(shape, dim):
    return lax.broadcasted_iota(jnp.int32, shape, dim)


def dot(left, right):
    return jnp.dot(left, right, preferred_element_type=F32)


def by_rows(left, weight):
    return lax.dot_general(left, weight, (((1,), (1,)), ((), ())), preferred_element_type=F32)


def layout(n, width):
    inner = 1
    while inner * inner < n:
        inner *= 2
    outer = n // inner
    pieces = max(1, TILE // outer)
    columns = width // pieces
    chunks = max(c for c in (1, 2, 3, 4) if (columns // 128) % c == 0)
    return inner, outer, pieces, columns, chunks


def kernel(
    n, slab_split,
    resid_h, query_h, key_h, value_h, decay_h, out_gate_h, norm_gain_h, moe_gain_h, ids_h, weights_h,
    state_h, w_out_h, w_gate_h, w_up_h, w_down_h,
    out,
    resid, query, key, value, decay, out_gate, norm_gain, moe_gain, ids, weights,
    state, w_out, w_gate, w_up, w_down,
    heads5, gains, hids, att3, recv1, send_a, recv_a, recv_r, recv_b, recv_d,
    recv_s, send_e, recv_e, send_f, recv_f,
    small_sem, load_sem, send_sem, recv_sem, *sems,
):
    heads, hdim = att3.shape[0], att3.shape[2]
    width = resid.shape[1]
    inner, outer, pieces, columns, chunks = layout(n, width)
    step = columns // chunks
    share = w_out_h.shape[0]
    me = lax.axis_index("wide")
    a, b = lax.div(me, inner), lax.rem(me, inner)
    tile = outer * pieces

    barrier = pltpu.get_barrier_semaphore()

    def greet(i, carry):
        pl.semaphore_signal(
            barrier, inc=1, device_id={"wide": lax.rem(me + i, n)},
            device_id_type=pl.DeviceIdType.MESH,
        )
        return carry

    small = []
    for i, (src, dst) in enumerate((
        (query_h, query), (key_h, key), (value_h, value), (out_gate_h, out_gate),
        (norm_gain_h, norm_gain), (decay_h, decay), (resid_h, resid),
        (moe_gain_h, moe_gain), (ids_h, ids), (weights_h, weights),
    )):
        small.append(pltpu.make_async_copy(src, dst, small_sem.at[i]))
        small[-1].start()
    part = state.shape[0] // STATE_CUTS
    loads = []
    for c in range(STATE_CUTS):
        at = pl.ds(c * part, part)
        loads.append(pltpu.make_async_copy(state_h.at[at], state.at[at], load_sem.at[c]))
        loads[-1].start()
    if share == hdim:
        get_out = pltpu.make_async_copy(w_out_h, w_out, load_sem.at[STATE_CUTS])
    else:
        w_out[...] = jnp.zeros_like(w_out)
        place = pl.ds(pl.multiple_of((me * share) % hdim, share), share)
        get_out = pltpu.make_async_copy(w_out_h, w_out.at[place], load_sem.at[STATE_CUTS])
    get_out.start()
    big = []
    for i, (src, dst) in enumerate(((w_gate_h, w_gate), (w_up_h, w_up), (w_down_h, w_down))):
        big.append(pltpu.make_async_copy(src.at[0], dst, load_sem.at[STATE_CUTS + 1 + i]))
        big[-1].start()

    lax.fori_loop(1, n, greet, 0)

    for copy in small:
        copy.wait()
    for i, ref in enumerate((query, key, value, out_gate, norm_gain)):
        line = ref[...].astype(F32)
        for h in range(heads):
            heads5[i, h : h + 1, :] = line[:, h * hdim : (h + 1) * hdim]
    line = resid[...].astype(F32)
    for p in range(pieces):
        recv_r[a, p : p + 1, :] = line[:, p * columns : (p + 1) * columns]
        for i in range(outer):
            at = i * pieces + p
            gains[at : at + 1, :] = moe_gain[:, p * columns : (p + 1) * columns]
    q, k, v = heads5[0], heads5[1], heads5[2]
    head_of = iota((heads, hdim), 0)
    eye = iota((heads, heads), 0) == iota((heads, heads), 1)
    fade = jnp.sum(
        jnp.where(eye, jnp.broadcast_to(jnp.exp(-decay[...]), (heads, heads)), 0.0),
        axis=1, keepdims=True,
    )
    att = jnp.zeros((heads, hdim), F32)
    per_cut = heads // STATE_CUTS
    for c in range(STATE_CUTS):
        diagonal = jnp.concatenate(
            [jnp.where(head_of == c * per_cut + h, q, 0.0).astype(BF16) for h in range(per_cut)],
            axis=1,
        )
        loads[c].wait()
        att += dot(diagonal, state[pl.ds(c * part, part), :].astype(BF16))
    att = fade * att + jnp.sum(q * k, axis=1, keepdims=True) * v
    mean = jnp.sum(jnp.sum(att * att, axis=1, keepdims=True), axis=0, keepdims=True) / (
        heads * hdim
    )
    attn = att * lax.rsqrt(mean + 1e-06) * heads5[4] * jax.nn.sigmoid(heads5[3])
    att3[...] = attn.reshape(heads, 1, hdim)

    pl.semaphore_wait(barrier, n - 1)

    slot = b * outer + a

    def head(device):
        return device if share == hdim else lax.div(device * share, hdim)

    for i in range(1, n):
        peer = lax.rem(me + i, n)
        pltpu.make_async_remote_copy(
            src_ref=att3.at[head(peer)], dst_ref=recv1.at[slot],
            send_sem=send_sem.at[0], recv_sem=recv_sem.at[0],
            device_id={"wide": peer}, device_id_type=pl.DeviceIdType.MESH,
        ).start()
    recv1[slot] = att3[head(me)]

    def settle(ref, count, sem):
        view = ref.at[pl.ds(0, count)]
        pltpu.make_async_copy(view, view, sem).wait()

    def to_inner(src, dst, ssem, rsem, pick):
        for i in range(1, inner):
            peer = lax.rem(b + i, inner)
            pltpu.make_async_remote_copy(
                src_ref=src.at[peer if pick else b], dst_ref=dst.at[b],
                send_sem=ssem, recv_sem=rsem,
                device_id={"wide": a * inner + peer}, device_id_type=pl.DeviceIdType.MESH,
            ).start()

    def to_outer(src, dst, ssem, rsem, pick):
        for i in range(1, outer):
            peer = lax.rem(a + i, outer)
            pltpu.make_async_remote_copy(
                src_ref=src.at[peer if pick else a], dst_ref=dst.at[a],
                send_sem=ssem, recv_sem=rsem,
                device_id={"wide": peer * inner + b}, device_id_type=pl.DeviceIdType.MESH,
            ).start()

    lines = n * pieces
    spread = (iota((lines, n), 0) // pieces == iota((lines, n), 1)).astype(F32).astype(BF16)
    piece_of = iota((lines, 1), 0) % pieces

    def only(p, full):
        return jnp.where(piece_of == p, full, 0.0).astype(BF16)

    owner = me // slab_split
    coef = jnp.sum(jnp.where(ids[...] == owner, weights[...], 0.0), axis=0, keepdims=True)
    line = iota((lines, n), 0) // pieces
    request = (line % outer) * inner + line // outer
    coef_line = jnp.sum(
        jnp.where(request == iota((lines, n), 1), jnp.broadcast_to(coef, (lines, n)), 0.0),
        axis=1, keepdims=True,
    )

    to_outer(recv_r, recv_r, send_sem.at[1], recv_sem.at[1], False)

    get_out.wait()
    settle(recv1, n - 1, recv_sem.at[0])
    full = dot(spread, recv1[...].reshape(n, hdim).astype(BF16))
    for c in range(chunks):
        proj = jnp.zeros((lines, step), F32)
        for p in range(pieces):
            start = p * columns + c * step
            proj += dot(only(p, full), w_out[:, start : start + step])
        send_a[c] = proj.astype(BF16).reshape(inner, tile, step)
        to_inner(send_a.at[c], recv_a.at[c], sems[0].at[c], sems[1].at[c], True)
        recv_a[c, b] = send_a[c, b]
    for c in range(chunks):
        settle(recv_a.at[c], inner - 1, sems[1].at[c])
        total = recv_a[c, 0].astype(F32)
        for i in range(1, inner):
            total += recv_a[c, i].astype(F32)
        recv_b[c, a] = total.astype(BF16)
        to_outer(recv_b.at[c], recv_b.at[c], sems[2].at[c], sems[3].at[c], False)
    settle(recv_r, outer - 1, recv_sem.at[1])
    squares = jnp.zeros((tile, 1), F32)
    for c in range(chunks):
        settle(recv_b.at[c], outer - 1, sems[3].at[c])
        total = recv_b[c, 0].astype(F32)
        for i in range(1, outer):
            total += recv_b[c, i].astype(F32)
        at = slice(c * step, (c + 1) * step)
        hid = (recv_r[:, :, at].reshape(tile, step) + total).astype(BF16).astype(F32)
        recv_d[c, b] = (hid * gains[:, at]).astype(BF16)
        to_inner(recv_d.at[c], recv_d.at[c], sems[4].at[c], sems[5].at[c], False)
        hids[c] = hid.reshape(outer, pieces, step)
        squares += jnp.sum(hid * hid, axis=1, keepdims=True)
    mates = iota((tile, outer), 0) // pieces == iota((tile, outer), 1)
    mean = jnp.sum(
        jnp.where(mates, jnp.broadcast_to(squares, (tile, outer)), 0.0), axis=0, keepdims=True
    ) / width
    same = iota((outer, outer), 0) == iota((outer, outer), 1)
    scale = jnp.sum(
        jnp.where(same, jnp.broadcast_to(lax.rsqrt(mean + 1e-06), (outer, outer)), 0.0),
        axis=1, keepdims=True,
    )
    recv_s[b] = jnp.broadcast_to(scale, (outer, hdim)).reshape(outer, 1, hdim)
    to_inner(recv_s, recv_s, send_sem.at[2], recv_sem.at[2], False)

    big[0].wait()
    big[1].wait()
    hidden = w_gate.shape[0]
    gate, upper = jnp.zeros((n, hidden), F32), jnp.zeros((n, hidden), F32)
    at_line = iota((n, lines), 0) * pieces
    for c in range(chunks):
        settle(recv_d.at[c], inner - 1, sems[5].at[c])
        part = recv_d[c].reshape(lines, step)
        for p in range(pieces):
            pick = (iota((n, lines), 1) == at_line + p).astype(F32).astype(BF16)
            x = dot(pick, part).astype(BF16)
            start = p * columns + c * step
            gate += by_rows(x, w_gate[:, start : start + step])
            upper += by_rows(x, w_up[:, start : start + step])
    settle(recv_s, inner - 1, recv_sem.at[2])
    scale = recv_s[...].reshape(n, hdim)[:, :1]
    gate, upper = gate * scale, upper * scale
    inner_act = (gate * jax.nn.sigmoid(gate) * upper).astype(BF16)
    full = dot(spread, inner_act)
    big[2].wait()
    for j in range(chunks):
        acc = jnp.zeros((lines, step), F32)
        for p in range(pieces):
            start = p * columns + j * step
            acc += dot(only(p, full), w_down[:, start : start + step])
        send_e[j] = (acc * coef_line).astype(BF16).reshape(inner, tile, step)
        to_inner(send_e.at[j], recv_e.at[j], sems[6].at[j], sems[7].at[j], True)
        recv_e[j, b] = send_e[j, b]
    for j in range(chunks):
        settle(recv_e.at[j], inner - 1, sems[7].at[j])
        total = recv_e[j, 0].astype(F32)
        for i in range(1, inner):
            total += recv_e[j, i].astype(F32)
        send_f[j] = total.reshape(outer, pieces, step)
        to_outer(send_f.at[j], recv_f.at[j], sems[8].at[j], sems[9].at[j], True)
        recv_f[j, a] = send_f[j, a]
    for j in range(chunks):
        settle(recv_f.at[j], outer - 1, sems[9].at[j])
        mixed = (hids[j, a] + jnp.sum(recv_f[j], axis=0)).astype(BF16)
        for p in range(pieces):
            start = p * columns + j * step
            out[:, start : start + step] = mixed[p : p + 1, :]

    settle(recv1, n - 1, send_sem.at[0])
    settle(recv_r, outer - 1, send_sem.at[1])
    settle(recv_s, inner - 1, send_sem.at[2])
    for j in range(chunks):
        settle(send_a.at[j], inner - 1, sems[0].at[j])
        settle(recv_b.at[j], outer - 1, sems[2].at[j])
        settle(recv_d.at[j], inner - 1, sems[4].at[j])
        settle(send_e.at[j], inner - 1, sems[6].at[j])
        settle(send_f.at[j], outer - 1, sems[8].at[j])


def shards(
    resid, query, key, value, state, decay, out_gate, norm_gain, w_out, moe_gain,
    w_gate, w_up, w_down, expert_ids, expert_weights, *, slab_split,
):
    n = lax.axis_size("wide")
    width = resid.shape[1]
    heads, hdim = state.shape[1], state.shape[2]
    inner, outer, pieces, columns, chunks = layout(n, width)
    step = columns // chunks
    tile = outer * pieces
    hidden = w_gate.shape[1]
    hbm = pl.BlockSpec(memory_space=pltpu.HBM)
    small = (
        resid, query, key, value, decay.reshape(1, -1), out_gate, norm_gain.reshape(1, -1),
        moe_gain.reshape(1, -1), expert_ids.T, expert_weights.T,
    )
    sems = pltpu.SemaphoreType.DMA
    return pl.pallas_call(
        functools.partial(kernel, n, slab_split),
        out_shape=jax.ShapeDtypeStruct(resid.shape, resid.dtype),
        in_specs=[hbm] * 15,
        out_specs=pl.BlockSpec(memory_space=pltpu.VMEM),
        scratch_shapes=[pltpu.VMEM(x.shape, x.dtype) for x in small] + [
            pltpu.VMEM((heads * hdim, hdim), F32),
            pltpu.VMEM((hdim, width), BF16),
            pltpu.VMEM((hidden, width), BF16),
            pltpu.VMEM((hidden, width), BF16),
            pltpu.VMEM((hidden, width), BF16),
            pltpu.VMEM((5, heads, hdim), F32),
            pltpu.VMEM((tile, columns), F32),
            pltpu.VMEM((chunks, outer, pieces, step), F32),
            pltpu.VMEM((heads, 1, hdim), F32),
            pltpu.VMEM((n, 1, hdim), F32),
            pltpu.VMEM((chunks, inner, tile, step), BF16),
            pltpu.VMEM((chunks, inner, tile, step), BF16),
            pltpu.VMEM((outer, pieces, columns), F32),
            pltpu.VMEM((chunks, outer, tile, step), BF16),
            pltpu.VMEM((chunks, inner, tile, step), BF16),
            pltpu.VMEM((inner, outer, 1, hdim), F32),
            pltpu.VMEM((chunks, inner, tile, step), BF16),
            pltpu.VMEM((chunks, inner, tile, step), BF16),
            pltpu.VMEM((chunks, outer, pieces, step), F32),
            pltpu.VMEM((chunks, outer, pieces, step), F32),
            sems((10,)),
            sems((STATE_CUTS + 4,)),
            sems((3,)),
            sems((3,)),
        ] + [sems((chunks,))] * 10,
        compiler_params=pltpu.CompilerParams(
            collective_id=0, has_side_effects=True, vmem_limit_bytes=VMEM
        ),
        name="decode_layer",
    )(
        *small,
        state.reshape(heads * hdim, hdim), w_out, w_gate, w_up, w_down,
    )


SPLIT = 8


def solution(mesh):
    rows = P(("group", "wide"), None)
    return jax.shard_map(
        functools.partial(shards, slab_split=SPLIT),
        mesh=mesh,
        in_specs=(
            rows, rows, rows, rows,
            P(("group", "wide"), None, None, None),
            P(), rows, P(), P("wide", None), P(),
            P("wide", None, None), P("wide", None, None), P("wide", None, None),
            P("group", None), P("group", None),
        ),
        out_specs=rows,
        check_vma=False,
    )
```

```python
import functools

import jax
import jax.numpy as jnp
from jax import lax
from jax.experimental import pallas as pl
from jax.experimental.pallas import tpu as pltpu
from jax.sharding import PartitionSpec as P

F32, BF16 = jnp.float32, jnp.bfloat16
TILE = 16
STATE_CUTS = 4
VMEM = 63 * 1024 * 1024


def iota(shape, dim):
    return lax.broadcasted_iota(jnp.int32, shape, dim)


def dot(left, right):
    return jnp.dot(left, right, preferred_element_type=F32)


def by_rows(left, weight):
    return lax.dot_general(left, weight, (((1,), (1,)), ((), ())), preferred_element_type=F32)


def layout(n, width):
    inner = 1
    while inner * inner < n:
        inner *= 2
    outer = n // inner
    pieces = max(1, TILE // outer)
    columns = width // pieces
    chunks = max(c for c in (1, 2, 3, 4) if (columns // 128) % c == 0)
    return inner, outer, pieces, columns, chunks


def kernel(
    n, slab_split,
    resid_h, query_h, key_h, value_h, decay_h, out_gate_h, norm_gain_h, moe_gain_h, ids_h, weights_h,
    state_h, w_out_h, w_gate_h, w_up_h, w_down_h,
    out,
    resid, query, key, value, decay, out_gate, norm_gain, moe_gain, ids, weights,
    state, w_out, w_gate, w_up, w_down,
    heads5, gains, hids, att3, recv1, send_a, recv_a, recv_r, recv_b, recv_d,
    recv_s, send_e, recv_e, send_f, recv_f,
    small_sem, load_sem, send_sem, recv_sem, *sems,
):
    heads, hdim = att3.shape[0], att3.shape[2]
    width = resid.shape[1]
    inner, outer, pieces, columns, chunks = layout(n, width)
    step = columns // chunks
    share = w_out_h.shape[0]
    me = lax.axis_index("wide")
    a, b = lax.div(me, inner), lax.rem(me, inner)
    tile = outer * pieces

    barrier = pltpu.get_barrier_semaphore()

    def greet(i, carry):
        pl.semaphore_signal(
            barrier, inc=1, device_id={"wide": lax.rem(me + i, n)},
            device_id_type=pl.DeviceIdType.MESH,
        )
        return carry

    small = []
    for i, (src, dst) in enumerate((
        (query_h, query), (key_h, key), (value_h, value), (out_gate_h, out_gate),
        (norm_gain_h, norm_gain), (decay_h, decay), (resid_h, resid),
        (moe_gain_h, moe_gain), (ids_h, ids), (weights_h, weights),
    )):
        small.append(pltpu.make_async_copy(src, dst, small_sem.at[i]))
        small[-1].start()
    part = state.shape[0] // STATE_CUTS
    loads = []
    for c in range(STATE_CUTS):
        at = pl.ds(c * part, part)
        loads.append(pltpu.make_async_copy(state_h.at[at], state.at[at], load_sem.at[c]))
        loads[-1].start()
    if share == hdim:
        get_out = pltpu.make_async_copy(w_out_h, w_out, load_sem.at[STATE_CUTS])
    else:
        w_out[...] = jnp.zeros_like(w_out)
        place = pl.ds(pl.multiple_of((me * share) % hdim, share), share)
        get_out = pltpu.make_async_copy(w_out_h, w_out.at[place], load_sem.at[STATE_CUTS])
    get_out.start()
    lax.fori_loop(1, n, greet, 0)

    for copy in small[:6]:
        copy.wait()
    for i, ref in enumerate((query, key, value, out_gate, norm_gain)):
        line = ref[...].astype(F32)
        for h in range(heads):
            heads5[i, h : h + 1, :] = line[:, h * hdim : (h + 1) * hdim]
    q, k, v = heads5[0], heads5[1], heads5[2]
    head_of = iota((heads, hdim), 0)
    eye = iota((heads, heads), 0) == iota((heads, heads), 1)
    fade = jnp.sum(
        jnp.where(eye, jnp.broadcast_to(jnp.exp(-decay[...]), (heads, heads)), 0.0),
        axis=1, keepdims=True,
    )
    att = jnp.zeros((heads, hdim), F32)
    per_cut = heads // STATE_CUTS
    for c in range(STATE_CUTS):
        diagonal = jnp.concatenate(
            [jnp.where(head_of == c * per_cut + h, q, 0.0).astype(BF16) for h in range(per_cut)],
            axis=1,
        )
        loads[c].wait()
        att += dot(diagonal, state[pl.ds(c * part, part), :].astype(BF16))
    att = fade * att + jnp.sum(q * k, axis=1, keepdims=True) * v
    mean = jnp.sum(jnp.sum(att * att, axis=1, keepdims=True), axis=0, keepdims=True) / (
        heads * hdim
    )
    attn = att * lax.rsqrt(mean + 1e-06) * heads5[4] * jax.nn.sigmoid(heads5[3])
    att3[...] = attn.reshape(heads, 1, hdim)

    pl.semaphore_wait(barrier, n - 1)

    slot = b * outer + a

    def head(device):
        return device if share == hdim else lax.div(device * share, hdim)

    for i in range(1, n):
        peer = lax.rem(me + i, n)
        pltpu.make_async_remote_copy(
            src_ref=att3.at[head(peer)], dst_ref=recv1.at[slot],
            send_sem=send_sem.at[0], recv_sem=recv_sem.at[0],
            device_id={"wide": peer}, device_id_type=pl.DeviceIdType.MESH,
        ).start()
    recv1[slot] = att3[head(me)]

    big = []
    for i, (src, dst) in enumerate(((w_gate_h, w_gate), (w_up_h, w_up), (w_down_h, w_down))):
        big.append(pltpu.make_async_copy(src.at[0], dst, load_sem.at[STATE_CUTS + 1 + i]))
        big[-1].start()

    def settle(ref, count, sem):
        view = ref.at[pl.ds(0, count)]
        pltpu.make_async_copy(view, view, sem).wait()

    def to_inner(src, dst, ssem, rsem, pick):
        for i in range(1, inner):
            peer = lax.rem(b + i, inner)
            pltpu.make_async_remote_copy(
                src_ref=src.at[peer if pick else b], dst_ref=dst.at[b],
                send_sem=ssem, recv_sem=rsem,
                device_id={"wide": a * inner + peer}, device_id_type=pl.DeviceIdType.MESH,
            ).start()

    def to_outer(src, dst, ssem, rsem, pick):
        for i in range(1, outer):
            peer = lax.rem(a + i, outer)
            pltpu.make_async_remote_copy(
                src_ref=src.at[peer if pick else a], dst_ref=dst.at[a],
                send_sem=ssem, recv_sem=rsem,
                device_id={"wide": peer * inner + b}, device_id_type=pl.DeviceIdType.MESH,
            ).start()

    for copy in small[6:]:
        copy.wait()

    lines = n * pieces
    spread = (iota((lines, n), 0) // pieces == iota((lines, n), 1)).astype(F32).astype(BF16)
    piece_of = iota((lines, 1), 0) % pieces

    def only(p, full):
        return jnp.where(piece_of == p, full, 0.0).astype(BF16)

    owner = me // slab_split
    coef = jnp.sum(jnp.where(ids[...] == owner, weights[...], 0.0), axis=0, keepdims=True)
    line = iota((lines, n), 0) // pieces
    request = (line % outer) * inner + line // outer
    coef_line = jnp.sum(
        jnp.where(request == iota((lines, n), 1), jnp.broadcast_to(coef, (lines, n)), 0.0),
        axis=1, keepdims=True,
    )

    line = resid[...].astype(F32)
    for p in range(pieces):
        recv_r[a, p : p + 1, :] = line[:, p * columns : (p + 1) * columns]
        for i in range(outer):
            at = i * pieces + p
            gains[at : at + 1, :] = moe_gain[:, p * columns : (p + 1) * columns]
    to_outer(recv_r, recv_r, send_sem.at[1], recv_sem.at[1], False)

    get_out.wait()
    settle(recv1, n - 1, recv_sem.at[0])
    full = dot(spread, recv1[...].reshape(n, hdim).astype(BF16))
    for c in range(chunks):
        proj = jnp.zeros((lines, step), F32)
        for p in range(pieces):
            start = p * columns + c * step
            proj += dot(only(p, full), w_out[:, start : start + step])
        send_a[c] = proj.astype(BF16).reshape(inner, tile, step)
        to_inner(send_a.at[c], recv_a.at[c], sems[0].at[c], sems[1].at[c], True)
        recv_a[c, b] = send_a[c, b]
    for c in range(chunks):
        settle(recv_a.at[c], inner - 1, sems[1].at[c])
        total = recv_a[c, 0].astype(F32)
        for i in range(1, inner):
            total += recv_a[c, i].astype(F32)
        recv_b[c, a] = total.astype(BF16)
        to_outer(recv_b.at[c], recv_b.at[c], sems[2].at[c], sems[3].at[c], False)
    settle(recv_r, outer - 1, recv_sem.at[1])
    squares = jnp.zeros((tile, 1), F32)
    for c in range(chunks):
        settle(recv_b.at[c], outer - 1, sems[3].at[c])
        total = recv_b[c, 0].astype(F32)
        for i in range(1, outer):
            total += recv_b[c, i].astype(F32)
        at = slice(c * step, (c + 1) * step)
        hid = (recv_r[:, :, at].reshape(tile, step) + total).astype(BF16).astype(F32)
        recv_d[c, b] = (hid * gains[:, at]).astype(BF16)
        to_inner(recv_d.at[c], recv_d.at[c], sems[4].at[c], sems[5].at[c], False)
        hids[c] = hid.reshape(outer, pieces, step)
        squares += jnp.sum(hid * hid, axis=1, keepdims=True)
    mates = iota((tile, outer), 0) // pieces == iota((tile, outer), 1)
    mean = jnp.sum(
        jnp.where(mates, jnp.broadcast_to(squares, (tile, outer)), 0.0), axis=0, keepdims=True
    ) / width
    same = iota((outer, outer), 0) == iota((outer, outer), 1)
    scale = jnp.sum(
        jnp.where(same, jnp.broadcast_to(lax.rsqrt(mean + 1e-06), (outer, outer)), 0.0),
        axis=1, keepdims=True,
    )
    recv_s[b] = jnp.broadcast_to(scale, (outer, hdim)).reshape(outer, 1, hdim)
    to_inner(recv_s, recv_s, send_sem.at[2], recv_sem.at[2], False)

    big[0].wait()
    big[1].wait()
    hidden = w_gate.shape[0]
    gate, upper = jnp.zeros((n, hidden), F32), jnp.zeros((n, hidden), F32)
    at_line = iota((n, lines), 0) * pieces
    for c in range(chunks):
        settle(recv_d.at[c], inner - 1, sems[5].at[c])
        part = recv_d[c].reshape(lines, step)
        for p in range(pieces):
            pick = (iota((n, lines), 1) == at_line + p).astype(F32).astype(BF16)
            x = dot(pick, part).astype(BF16)
            start = p * columns + c * step
            gate += by_rows(x, w_gate[:, start : start + step])
            upper += by_rows(x, w_up[:, start : start + step])
    settle(recv_s, inner - 1, recv_sem.at[2])
    scale = recv_s[...].reshape(n, hdim)[:, :1]
    gate, upper = gate * scale, upper * scale
    inner_act = (gate * jax.nn.sigmoid(gate) * upper).astype(BF16)
    full = dot(spread, inner_act)
    big[2].wait()
    for j in range(chunks):
        acc = jnp.zeros((lines, step), F32)
        for p in range(pieces):
            start = p * columns + j * step
            acc += dot(only(p, full), w_down[:, start : start + step])
        send_e[j] = (acc * coef_line).astype(BF16).reshape(inner, tile, step)
        to_inner(send_e.at[j], recv_e.at[j], sems[6].at[j], sems[7].at[j], True)
        recv_e[j, b] = send_e[j, b]
    for j in range(chunks):
        settle(recv_e.at[j], inner - 1, sems[7].at[j])
        total = recv_e[j, 0].astype(F32)
        for i in range(1, inner):
            total += recv_e[j, i].astype(F32)
        send_f[j] = total.reshape(outer, pieces, step)
        to_outer(send_f.at[j], recv_f.at[j], sems[8].at[j], sems[9].at[j], True)
        recv_f[j, a] = send_f[j, a]
    for j in range(chunks):
        settle(recv_f.at[j], outer - 1, sems[9].at[j])
        mixed = (hids[j, a] + jnp.sum(recv_f[j], axis=0)).astype(BF16)
        for p in range(pieces):
            start = p * columns + j * step
            out[:, start : start + step] = mixed[p : p + 1, :]

    settle(recv1, n - 1, send_sem.at[0])
    settle(recv_r, outer - 1, send_sem.at[1])
    settle(recv_s, inner - 1, send_sem.at[2])
    for j in range(chunks):
        settle(send_a.at[j], inner - 1, sems[0].at[j])
        settle(recv_b.at[j], outer - 1, sems[2].at[j])
        settle(recv_d.at[j], inner - 1, sems[4].at[j])
        settle(send_e.at[j], inner - 1, sems[6].at[j])
        settle(send_f.at[j], outer - 1, sems[8].at[j])


def shards(
    resid, query, key, value, state, decay, out_gate, norm_gain, w_out, moe_gain,
    w_gate, w_up, w_down, expert_ids, expert_weights, *, slab_split,
):
    n = lax.axis_size("wide")
    width = resid.shape[1]
    heads, hdim = state.shape[1], state.shape[2]
    inner, outer, pieces, columns, chunks = layout(n, width)
    step = columns // chunks
    tile = outer * pieces
    hidden = w_gate.shape[1]
    hbm = pl.BlockSpec(memory_space=pltpu.HBM)
    small = (
        resid, query, key, value, decay.reshape(1, -1), out_gate, norm_gain.reshape(1, -1),
        moe_gain.reshape(1, -1), expert_ids.T, expert_weights.T,
    )
    sems = pltpu.SemaphoreType.DMA
    return pl.pallas_call(
        functools.partial(kernel, n, slab_split),
        out_shape=pltpu.VMEM(resid.shape, resid.dtype),
        in_specs=[hbm] * 15,
        out_specs=pl.BlockSpec(memory_space=pltpu.VMEM),
        scratch_shapes=[pltpu.VMEM(x.shape, x.dtype) for x in small] + [
            pltpu.VMEM((heads * hdim, hdim), F32),
            pltpu.VMEM((hdim, width), BF16),
            pltpu.VMEM((hidden, width), BF16),
            pltpu.VMEM((hidden, width), BF16),
            pltpu.VMEM((hidden, width), BF16),
            pltpu.VMEM((5, heads, hdim), F32),
            pltpu.VMEM((tile, columns), F32),
            pltpu.VMEM((chunks, outer, pieces, step), F32),
            pltpu.VMEM((heads, 1, hdim), F32),
            pltpu.VMEM((n, 1, hdim), F32),
            pltpu.VMEM((chunks, inner, tile, step), BF16),
            pltpu.VMEM((chunks, inner, tile, step), BF16),
            pltpu.VMEM((outer, pieces, columns), F32),
            pltpu.VMEM((chunks, outer, tile, step), BF16),
            pltpu.VMEM((chunks, inner, tile, step), BF16),
            pltpu.VMEM((inner, outer, 1, hdim), F32),
            pltpu.VMEM((chunks, inner, tile, step), BF16),
            pltpu.VMEM((chunks, inner, tile, step), BF16),
            pltpu.VMEM((chunks, outer, pieces, step), F32),
            pltpu.VMEM((chunks, outer, pieces, step), F32),
            sems((10,)),
            sems((STATE_CUTS + 4,)),
            sems((3,)),
            sems((3,)),
        ] + [sems((chunks,))] * 10,
        compiler_params=pltpu.CompilerParams(
            collective_id=0, has_side_effects=True, vmem_limit_bytes=VMEM
        ),
        name="decode_layer",
    )(
        *small,
        state.reshape(heads * hdim, hdim), w_out, w_gate, w_up, w_down,
    )


SPLIT = 8


def solution(mesh):
    rows = P(("group", "wide"), None)
    return jax.shard_map(
        functools.partial(shards, slab_split=SPLIT),
        mesh=mesh,
        in_specs=(
            rows, rows, rows, rows,
            P(("group", "wide"), None, None, None),
            P(), rows, P(), P("wide", None), P(),
            P("wide", None, None), P("wide", None, None), P("wide", None, None),
            P("group", None), P("group", None),
        ),
        out_specs=rows,
        check_vma=False,
    )
```

```python
import functools

import jax
import jax.numpy as jnp
from jax import lax
from jax.experimental import pallas as pl
from jax.experimental.pallas import tpu as pltpu
from jax.sharding import PartitionSpec as P

F32, BF16 = jnp.float32, jnp.bfloat16
TILE = 16
STATE_CUTS = 4
VMEM = 63 * 1024 * 1024


def iota(shape, dim):
    return lax.broadcasted_iota(jnp.int32, shape, dim)


def dot(left, right):
    return jnp.dot(left, right, preferred_element_type=F32)


def by_rows(left, weight):
    return lax.dot_general(left, weight, (((1,), (1,)), ((), ())), preferred_element_type=F32)


def layout(n, width):
    inner = 1
    while inner * inner < n:
        inner *= 2
    outer = n // inner
    pieces = max(1, TILE // outer)
    columns = width // pieces
    chunks = max(c for c in (1, 2, 3, 4) if (columns // 128) % c == 0)
    return inner, outer, pieces, columns, chunks


def kernel(
    n, slab_split,
    resid_h, query_h, key_h, value_h, decay_h, out_gate_h, norm_gain_h, moe_gain_h, ids_h, weights_h,
    state_h, w_out_h, w_gate_h, w_up_h, w_down_h,
    out,
    resid, query, key, value, decay, out_gate, norm_gain, moe_gain, ids, weights,
    state, w_out, w_gate, w_up, w_down,
    heads5, gains, hids, att3, recv1, send_a, recv_a, recv_r, recv_b, recv_d,
    recv_s, send_e, recv_e, send_f, recv_f,
    small_sem, load_sem, send_sem, recv_sem, *sems,
):
    heads, hdim = att3.shape[0], att3.shape[2]
    width = resid.shape[1]
    inner, outer, pieces, columns, chunks = layout(n, width)
    step = columns // chunks
    share = w_out_h.shape[0]
    me = lax.axis_index("wide")
    a, b = lax.div(me, inner), lax.rem(me, inner)
    tile = outer * pieces

    barrier = pltpu.get_barrier_semaphore()

    def greet(i, carry):
        pl.semaphore_signal(
            barrier, inc=1, device_id={"wide": lax.rem(me + i, n)},
            device_id_type=pl.DeviceIdType.MESH,
        )
        return carry

    small = []
    for i, (src, dst) in enumerate((
        (query_h, query), (key_h, key), (value_h, value), (out_gate_h, out_gate),
        (norm_gain_h, norm_gain), (decay_h, decay), (resid_h, resid),
        (moe_gain_h, moe_gain), (ids_h, ids), (weights_h, weights),
    )):
        small.append(pltpu.make_async_copy(src, dst, small_sem.at[i]))
        small[-1].start()
    part = state.shape[0] // STATE_CUTS
    loads = []
    for c in range(STATE_CUTS):
        at = pl.ds(c * part, part)
        loads.append(pltpu.make_async_copy(state_h.at[at], state.at[at], load_sem.at[c]))
        loads[-1].start()
    if share == hdim:
        get_out = pltpu.make_async_copy(w_out_h, w_out, load_sem.at[STATE_CUTS])
    else:
        w_out[...] = jnp.zeros_like(w_out)
        place = pl.ds(pl.multiple_of((me * share) % hdim, share), share)
        get_out = pltpu.make_async_copy(w_out_h, w_out.at[place], load_sem.at[STATE_CUTS])
    get_out.start()
    lax.fori_loop(1, n, greet, 0)

    for copy in small[:6]:
        copy.wait()
    for i, ref in enumerate((query, key, value, out_gate, norm_gain)):
        line = ref[...].astype(F32)
        for h in range(heads):
            heads5[i, h : h + 1, :] = line[:, h * hdim : (h + 1) * hdim]
    q, k, v = heads5[0], heads5[1], heads5[2]
    eye = iota((heads, heads), 0) == iota((heads, heads), 1)
    fade = jnp.sum(
        jnp.where(eye, jnp.broadcast_to(jnp.exp(-decay[...]), (heads, heads)), 0.0),
        axis=1, keepdims=True,
    )
    slot = b * outer + a

    def head(device):
        return device if share == hdim else lax.div(device * share, hdim)

    def send_head(peer):
        pltpu.make_async_remote_copy(
            src_ref=att3.at[head(peer)], dst_ref=recv1.at[slot],
            send_sem=send_sem.at[0], recv_sem=recv_sem.at[0],
            device_id={"wide": peer}, device_id_type=pl.DeviceIdType.MESH,
        ).start()

    per_cut, holders = heads // STATE_CUTS, n // STATE_CUTS
    squares = jnp.zeros((per_cut, 1), F32)
    for c in range(STATE_CUTS):
        at = slice(c * per_cut, (c + 1) * per_cut)
        q_c = q[at]
        row = iota((per_cut, hdim), 0)
        diagonal = jnp.concatenate(
            [jnp.where(row == h, q_c, 0.0) for h in range(per_cut)], axis=1
        ).astype(BF16)
        loads[c].wait()
        att = dot(diagonal, state[pl.ds(c * part, part), :].astype(BF16))
        att = fade[at] * att + jnp.sum(q_c * k[at], axis=1, keepdims=True) * v[at]
        squares += jnp.sum(att * att, axis=1, keepdims=True)
        attn = att * heads5[4, at, :] * jax.nn.sigmoid(heads5[3, at, :])
        att3[at] = attn.reshape(per_cut, 1, hdim)
        if c == 0:
            pl.semaphore_wait(barrier, n - 1)
        first = c * holders + lax.rem(me, holders)
        pl.when(first != me)(functools.partial(send_head, first))
        for i in range(1, holders):
            send_head(c * holders + lax.rem(me + i, holders))
    recv1[slot] = att3[head(me)]
    mean = jnp.sum(squares, axis=0, keepdims=True) / (heads * hdim)
    scale = lax.rsqrt(mean + 1e-06)

    big = []
    for i, (src, dst) in enumerate(((w_gate_h, w_gate), (w_up_h, w_up), (w_down_h, w_down))):
        big.append(pltpu.make_async_copy(src.at[0], dst, load_sem.at[STATE_CUTS + 1 + i]))

    big[0].start()

    def settle(ref, count, sem):
        view = ref.at[pl.ds(0, count)]
        pltpu.make_async_copy(view, view, sem).wait()

    def to_inner(src, dst, ssem, rsem, pick):
        for i in range(1, inner):
            peer = lax.rem(b + i, inner)
            pltpu.make_async_remote_copy(
                src_ref=src.at[peer if pick else b], dst_ref=dst.at[b],
                send_sem=ssem, recv_sem=rsem,
                device_id={"wide": a * inner + peer}, device_id_type=pl.DeviceIdType.MESH,
            ).start()

    def to_outer(src, dst, ssem, rsem, pick):
        for i in range(1, outer):
            peer = lax.rem(a + i, outer)
            pltpu.make_async_remote_copy(
                src_ref=src.at[peer if pick else a], dst_ref=dst.at[a],
                send_sem=ssem, recv_sem=rsem,
                device_id={"wide": peer * inner + b}, device_id_type=pl.DeviceIdType.MESH,
            ).start()

    for copy in small[6:]:
        copy.wait()

    lines = n * pieces
    spread = (iota((lines, n), 0) // pieces == iota((lines, n), 1)).astype(F32).astype(BF16)
    piece_of = iota((lines, 1), 0) % pieces

    def only(p, full):
        return jnp.where(piece_of == p, full, 0.0).astype(BF16)

    owner = me // slab_split
    coef = jnp.sum(jnp.where(ids[...] == owner, weights[...], 0.0), axis=0, keepdims=True)
    line = iota((lines, n), 0) // pieces
    request = (line % outer) * inner + line // outer
    coef_line = jnp.sum(
        jnp.where(request == iota((lines, n), 1), jnp.broadcast_to(coef, (lines, n)), 0.0),
        axis=1, keepdims=True,
    )

    recv_r[a, pieces : pieces + 1, :] = jnp.broadcast_to(scale, (1, columns))
    line = resid[...].astype(F32)
    for p in range(pieces):
        recv_r[a, p : p + 1, :] = line[:, p * columns : (p + 1) * columns]
        for i in range(outer):
            at = i * pieces + p
            gains[at : at + 1, :] = moe_gain[:, p * columns : (p + 1) * columns]
    to_outer(recv_r, recv_r, send_sem.at[1], recv_sem.at[1], False)

    get_out.wait()
    settle(recv1, n - 1, recv_sem.at[0])
    full = dot(spread, recv1[...].reshape(n, hdim).astype(BF16))
    for c in range(chunks):
        proj = jnp.zeros((lines, step), F32)
        for p in range(pieces):
            start = p * columns + c * step
            proj += dot(only(p, full), w_out[:, start : start + step])
        send_a[c] = proj.astype(BF16).reshape(inner, tile, step)
        to_inner(send_a.at[c], recv_a.at[c], sems[0].at[c], sems[1].at[c], True)
        recv_a[c, b] = send_a[c, b]
    big[1].start()
    for c in range(chunks):
        settle(recv_a.at[c], inner - 1, sems[1].at[c])
        total = recv_a[c, 0].astype(F32)
        for i in range(1, inner):
            total += recv_a[c, i].astype(F32)
        recv_b[c, a] = total.astype(BF16)
        to_outer(recv_b.at[c], recv_b.at[c], sems[2].at[c], sems[3].at[c], False)
    big[2].start()
    settle(recv_r, outer - 1, recv_sem.at[1])
    scale = jnp.broadcast_to(
        recv_r[:, pieces : pieces + 1, :step], (outer, pieces, step)
    ).reshape(tile, step)
    squares = jnp.zeros((tile, 1), F32)
    for c in range(chunks):
        settle(recv_b.at[c], outer - 1, sems[3].at[c])
        total = recv_b[c, 0].astype(F32)
        for i in range(1, outer):
            total += recv_b[c, i].astype(F32)
        at = slice(c * step, (c + 1) * step)
        hid = (recv_r[:, :pieces, at].reshape(tile, step) + total * scale).astype(BF16).astype(F32)
        recv_d[c, b] = (hid * gains[:, at]).astype(BF16)
        to_inner(recv_d.at[c], recv_d.at[c], sems[4].at[c], sems[5].at[c], False)
        hids[c] = hid.reshape(outer, pieces, step)
        squares += jnp.sum(hid * hid, axis=1, keepdims=True)
    mates = iota((tile, outer), 0) // pieces == iota((tile, outer), 1)
    mean = jnp.sum(
        jnp.where(mates, jnp.broadcast_to(squares, (tile, outer)), 0.0), axis=0, keepdims=True
    ) / width
    same = iota((outer, outer), 0) == iota((outer, outer), 1)
    scale = jnp.sum(
        jnp.where(same, jnp.broadcast_to(lax.rsqrt(mean + 1e-06), (outer, outer)), 0.0),
        axis=1, keepdims=True,
    )
    recv_s[b] = jnp.broadcast_to(scale, (outer, hdim)).reshape(outer, 1, hdim)
    to_inner(recv_s, recv_s, send_sem.at[2], recv_sem.at[2], False)

    big[0].wait()
    big[1].wait()
    hidden = w_gate.shape[0]
    gate, upper = jnp.zeros((n, hidden), F32), jnp.zeros((n, hidden), F32)
    at_line = iota((n, lines), 0) * pieces
    for c in range(chunks):
        settle(recv_d.at[c], inner - 1, sems[5].at[c])
        part = recv_d[c].reshape(lines, step)
        for p in range(pieces):
            pick = (iota((n, lines), 1) == at_line + p).astype(F32).astype(BF16)
            x = dot(pick, part).astype(BF16)
            start = p * columns + c * step
            gate += by_rows(x, w_gate[:, start : start + step])
            upper += by_rows(x, w_up[:, start : start + step])
    settle(recv_s, inner - 1, recv_sem.at[2])
    scale = recv_s[...].reshape(n, hdim)[:, :1]
    gate, upper = gate * scale, upper * scale
    inner_act = (gate * jax.nn.sigmoid(gate) * upper).astype(BF16)
    full = dot(spread, inner_act)
    big[2].wait()
    for j in range(chunks):
        acc = jnp.zeros((lines, step), F32)
        for p in range(pieces):
            start = p * columns + j * step
            acc += dot(only(p, full), w_down[:, start : start + step])
        send_e[j] = (acc * coef_line).astype(BF16).reshape(inner, tile, step)
        to_inner(send_e.at[j], recv_e.at[j], sems[6].at[j], sems[7].at[j], True)
        recv_e[j, b] = send_e[j, b]
    for j in range(chunks):
        settle(recv_e.at[j], inner - 1, sems[7].at[j])
        total = recv_e[j, 0].astype(F32)
        for i in range(1, inner):
            total += recv_e[j, i].astype(F32)
        send_f[j] = total.reshape(outer, pieces, step)
        to_outer(send_f.at[j], recv_f.at[j], sems[8].at[j], sems[9].at[j], True)
        recv_f[j, a] = send_f[j, a]
    for j in range(chunks):
        settle(recv_f.at[j], outer - 1, sems[9].at[j])
        mixed = (hids[j, a] + jnp.sum(recv_f[j], axis=0)).astype(BF16)
        for p in range(pieces):
            start = p * columns + j * step
            out[:, start : start + step] = mixed[p : p + 1, :]

    settle(recv1, n - 1, send_sem.at[0])
    settle(recv_r, outer - 1, send_sem.at[1])
    settle(recv_s, inner - 1, send_sem.at[2])
    for j in range(chunks):
        settle(send_a.at[j], inner - 1, sems[0].at[j])
        settle(recv_b.at[j], outer - 1, sems[2].at[j])
        settle(recv_d.at[j], inner - 1, sems[4].at[j])
        settle(send_e.at[j], inner - 1, sems[6].at[j])
        settle(send_f.at[j], outer - 1, sems[8].at[j])


def shards(
    resid, query, key, value, state, decay, out_gate, norm_gain, w_out, moe_gain,
    w_gate, w_up, w_down, expert_ids, expert_weights, *, slab_split,
):
    n = lax.axis_size("wide")
    width = resid.shape[1]
    heads, hdim = state.shape[1], state.shape[2]
    inner, outer, pieces, columns, chunks = layout(n, width)
    step = columns // chunks
    tile = outer * pieces
    hidden = w_gate.shape[1]
    hbm = pl.BlockSpec(memory_space=pltpu.HBM)
    small = (
        resid, query, key, value, decay.reshape(1, -1), out_gate, norm_gain.reshape(1, -1),
        moe_gain.reshape(1, -1), expert_ids.T, expert_weights.T,
    )
    sems = pltpu.SemaphoreType.DMA
    return pl.pallas_call(
        functools.partial(kernel, n, slab_split),
        out_shape=pltpu.VMEM(resid.shape, resid.dtype),
        in_specs=[hbm] * 15,
        out_specs=pl.BlockSpec(memory_space=pltpu.VMEM),
        scratch_shapes=[pltpu.VMEM(x.shape, x.dtype) for x in small] + [
            pltpu.VMEM((heads * hdim, hdim), F32),
            pltpu.VMEM((hdim, width), BF16),
            pltpu.VMEM((hidden, width), BF16),
            pltpu.VMEM((hidden, width), BF16),
            pltpu.VMEM((hidden, width), BF16),
            pltpu.VMEM((5, heads, hdim), F32),
            pltpu.VMEM((tile, columns), F32),
            pltpu.VMEM((chunks, outer, pieces, step), F32),
            pltpu.VMEM((heads, 1, hdim), F32),
            pltpu.VMEM((n, 1, hdim), F32),
            pltpu.VMEM((chunks, inner, tile, step), BF16),
            pltpu.VMEM((chunks, inner, tile, step), BF16),
            pltpu.VMEM((outer, pieces + 1, columns), F32),
            pltpu.VMEM((chunks, outer, tile, step), BF16),
            pltpu.VMEM((chunks, inner, tile, step), BF16),
            pltpu.VMEM((inner, outer, 1, hdim), F32),
            pltpu.VMEM((chunks, inner, tile, step), BF16),
            pltpu.VMEM((chunks, inner, tile, step), BF16),
            pltpu.VMEM((chunks, outer, pieces, step), F32),
            pltpu.VMEM((chunks, outer, pieces, step), F32),
            sems((10,)),
            sems((STATE_CUTS + 4,)),
            sems((3,)),
            sems((3,)),
        ] + [sems((chunks,))] * 10,
        compiler_params=pltpu.CompilerParams(
            collective_id=0, has_side_effects=True, vmem_limit_bytes=VMEM
        ),
        name="decode_layer",
    )(
        *small,
        state.reshape(heads * hdim, hdim), w_out, w_gate, w_up, w_down,
    )


SPLIT = 8


def solution(mesh):
    rows = P(("group", "wide"), None)
    return jax.shard_map(
        functools.partial(shards, slab_split=SPLIT),
        mesh=mesh,
        in_specs=(
            rows, rows, rows, rows,
            P(("group", "wide"), None, None, None),
            P(), rows, P(), P("wide", None), P(),
            P("wide", None, None), P("wide", None, None), P("wide", None, None),
            P("group", None), P("group", None),
        ),
        out_specs=rows,
        check_vma=False,
    )
```

```python
import functools

import jax
import jax.numpy as jnp
from jax import lax
from jax.experimental import pallas as pl
from jax.experimental.pallas import tpu as pltpu
from jax.sharding import PartitionSpec as P

F32, BF16 = jnp.float32, jnp.bfloat16
TILE = 16
STATE_CUTS = 4
VMEM = 63 * 1024 * 1024


def iota(shape, dim):
    return lax.broadcasted_iota(jnp.int32, shape, dim)


def dot(left, right):
    return jnp.dot(left, right, preferred_element_type=F32)


def by_rows(left, weight):
    return lax.dot_general(left, weight, (((1,), (1,)), ((), ())), preferred_element_type=F32)


def layout(n, width):
    inner = 1
    while inner * inner < n:
        inner *= 2
    outer = n // inner
    pieces = max(1, TILE // outer)
    columns = width // pieces
    chunks = max(c for c in (1, 2, 3, 4) if (columns // 128) % c == 0)
    return inner, outer, pieces, columns, chunks


def kernel(
    n, slab_split,
    resid_h, query_h, key_h, value_h, decay_h, out_gate_h, norm_gain_h, moe_gain_h, ids_h, weights_h,
    state_h, w_out_h, w_gate_h, w_up_h, w_down_h,
    out,
    resid, query, key, value, decay, out_gate, norm_gain, moe_gain, ids, weights,
    state, w_out, w_gate, w_up, w_down,
    heads5, gains, hids, att3, recv1, send_a, recv_a, recv_r, recv_b, recv_d,
    recv_s, send_e, recv_e, send_f, recv_f,
    small_sem, load_sem, send_sem, recv_sem, *sems,
):
    heads, hdim = att3.shape[0], att3.shape[2]
    width = resid.shape[1]
    inner, outer, pieces, columns, chunks = layout(n, width)
    step = columns // chunks
    share = w_out_h.shape[0]
    me = lax.axis_index("wide")
    a, b = lax.div(me, inner), lax.rem(me, inner)
    tile = outer * pieces

    barrier = pltpu.get_barrier_semaphore()

    def greet(i, carry):
        pl.semaphore_signal(
            barrier, inc=1, device_id={"wide": lax.rem(me + i, n)},
            device_id_type=pl.DeviceIdType.MESH,
        )
        return carry

    small = []
    for i, (src, dst) in enumerate((
        (query_h, query), (key_h, key), (value_h, value), (out_gate_h, out_gate),
        (norm_gain_h, norm_gain), (decay_h, decay), (resid_h, resid),
        (moe_gain_h, moe_gain), (ids_h, ids), (weights_h, weights),
    )):
        small.append(pltpu.make_async_copy(src, dst, small_sem.at[i]))
        small[-1].start()
    part = state.shape[0] // STATE_CUTS
    loads = []
    for c in range(STATE_CUTS):
        at = pl.ds(c * part, part)
        loads.append(pltpu.make_async_copy(state_h.at[at], state.at[at], load_sem.at[c]))
        loads[-1].start()
    if share == hdim:
        get_out = pltpu.make_async_copy(w_out_h, w_out, load_sem.at[STATE_CUTS])
    else:
        w_out[...] = jnp.zeros_like(w_out)
        place = pl.ds(pl.multiple_of((me * share) % hdim, share), share)
        get_out = pltpu.make_async_copy(w_out_h, w_out.at[place], load_sem.at[STATE_CUTS])
    get_out.start()
    lax.fori_loop(1, n, greet, 0)

    for copy in small[:6]:
        copy.wait()
    for i, ref in enumerate((query, key, value, out_gate, norm_gain)):
        line = ref[...].astype(F32)
        for h in range(heads):
            heads5[i, h : h + 1, :] = line[:, h * hdim : (h + 1) * hdim]
    q, k, v = heads5[0], heads5[1], heads5[2]
    eye = iota((heads, heads), 0) == iota((heads, heads), 1)
    fade = jnp.sum(
        jnp.where(eye, jnp.broadcast_to(jnp.exp(-decay[...]), (heads, heads)), 0.0),
        axis=1, keepdims=True,
    )
    per_cut = heads // STATE_CUTS
    row = iota((per_cut, hdim), 0)
    cuts = []
    for c in range(STATE_CUTS):
        q_c = q[c * per_cut : (c + 1) * per_cut]
        diagonal = jnp.concatenate(
            [jnp.where(row == h, q_c, 0.0) for h in range(per_cut)], axis=1
        ).astype(BF16)
        loads[c].wait()
        cuts.append(dot(diagonal, state[pl.ds(c * part, part), :].astype(BF16)))
    att = jnp.concatenate(cuts, axis=0)
    att = fade * att + jnp.sum(q * k, axis=1, keepdims=True) * v
    mean = jnp.sum(jnp.sum(att * att, axis=1, keepdims=True), axis=0, keepdims=True) / (
        heads * hdim
    )
    attn = att * lax.rsqrt(mean + 1e-06) * heads5[4] * jax.nn.sigmoid(heads5[3])
    att3[...] = attn.reshape(heads, 1, hdim)

    pl.semaphore_wait(barrier, n - 1)

    slot = b * outer + a

    def head(device):
        return device if share == hdim else lax.div(device * share, hdim)

    for i in range(1, n):
        peer = lax.rem(me + i, n)
        pltpu.make_async_remote_copy(
            src_ref=att3.at[head(peer)], dst_ref=recv1.at[slot],
            send_sem=send_sem.at[0], recv_sem=recv_sem.at[0],
            device_id={"wide": peer}, device_id_type=pl.DeviceIdType.MESH,
        ).start()
    recv1[slot] = att3[head(me)]

    big = []
    for i, (src, dst) in enumerate(((w_gate_h, w_gate), (w_up_h, w_up), (w_down_h, w_down))):
        big.append(pltpu.make_async_copy(src.at[0], dst, load_sem.at[STATE_CUTS + 1 + i]))
        big[-1].start()

    def settle(ref, count, sem):
        view = ref.at[pl.ds(0, count)]
        pltpu.make_async_copy(view, view, sem).wait()

    def to_inner(src, dst, ssem, rsem, pick):
        for i in range(1, inner):
            peer = lax.rem(b + i, inner)
            pltpu.make_async_remote_copy(
                src_ref=src.at[peer if pick else b], dst_ref=dst.at[b],
                send_sem=ssem, recv_sem=rsem,
                device_id={"wide": a * inner + peer}, device_id_type=pl.DeviceIdType.MESH,
            ).start()

    def to_outer(src, dst, ssem, rsem, pick):
        for i in range(1, outer):
            peer = lax.rem(a + i, outer)
            pltpu.make_async_remote_copy(
                src_ref=src.at[peer if pick else a], dst_ref=dst.at[a],
                send_sem=ssem, recv_sem=rsem,
                device_id={"wide": peer * inner + b}, device_id_type=pl.DeviceIdType.MESH,
            ).start()

    for copy in small[6:]:
        copy.wait()

    lines = n * pieces
    spread = (iota((lines, n), 0) // pieces == iota((lines, n), 1)).astype(F32).astype(BF16)
    piece_of = iota((lines, 1), 0) % pieces

    def only(p, full):
        return jnp.where(piece_of == p, full, 0.0).astype(BF16)

    owner = me // slab_split
    coef = jnp.sum(jnp.where(ids[...] == owner, weights[...], 0.0), axis=0, keepdims=True)
    line = iota((n, n), 0)
    request = lax.rem(line, outer) * inner + lax.div(line, outer)
    coef = jnp.sum(
        jnp.where(request == iota((n, n), 1), jnp.broadcast_to(coef, (n, n)), 0.0),
        axis=1, keepdims=True,
    )

    line = resid[...].astype(F32)
    for p in range(pieces):
        recv_r[a, p : p + 1, :] = line[:, p * columns : (p + 1) * columns]
        for i in range(outer):
            at = i * pieces + p
            gains[at : at + 1, :] = moe_gain[:, p * columns : (p + 1) * columns]
    to_outer(recv_r, recv_r, send_sem.at[1], recv_sem.at[1], False)

    get_out.wait()
    settle(recv1, n - 1, recv_sem.at[0])
    full = dot(spread, recv1[...].reshape(n, hdim).astype(BF16))
    for c in range(chunks):
        proj = jnp.zeros((lines, step), F32)
        for p in range(pieces):
            start = p * columns + c * step
            proj += dot(only(p, full), w_out[:, start : start + step])
        send_a[c] = proj.astype(BF16).reshape(inner, tile, step)
        to_inner(send_a.at[c], recv_a.at[c], sems[0].at[c], sems[1].at[c], True)
        recv_a[c, b] = send_a[c, b]
    for c in range(chunks):
        settle(recv_a.at[c], inner - 1, sems[1].at[c])
        total = recv_a[c, 0].astype(F32)
        for i in range(1, inner):
            total += recv_a[c, i].astype(F32)
        recv_b[c, a] = total.astype(BF16)
        to_outer(recv_b.at[c], recv_b.at[c], sems[2].at[c], sems[3].at[c], False)
    settle(recv_r, outer - 1, recv_sem.at[1])
    squares = jnp.zeros((tile, 1), F32)
    for c in range(chunks):
        settle(recv_b.at[c], outer - 1, sems[3].at[c])
        total = recv_b[c, 0].astype(F32)
        for i in range(1, outer):
            total += recv_b[c, i].astype(F32)
        at = slice(c * step, (c + 1) * step)
        hid = (recv_r[:, :, at].reshape(tile, step) + total).astype(BF16).astype(F32)
        recv_d[c, b] = (hid * gains[:, at]).astype(BF16)
        to_inner(recv_d.at[c], recv_d.at[c], sems[4].at[c], sems[5].at[c], False)
        hids[c] = hid.reshape(outer, pieces, step)
        squares += jnp.sum(hid * hid, axis=1, keepdims=True)
    mates = iota((tile, outer), 0) // pieces == iota((tile, outer), 1)
    mean = jnp.sum(
        jnp.where(mates, jnp.broadcast_to(squares, (tile, outer)), 0.0), axis=0, keepdims=True
    ) / width
    same = iota((outer, outer), 0) == iota((outer, outer), 1)
    scale = jnp.sum(
        jnp.where(same, jnp.broadcast_to(lax.rsqrt(mean + 1e-06), (outer, outer)), 0.0),
        axis=1, keepdims=True,
    )
    recv_s[b] = jnp.broadcast_to(scale, (outer, hdim)).reshape(outer, 1, hdim)
    to_inner(recv_s, recv_s, send_sem.at[2], recv_sem.at[2], False)

    big[0].wait()
    big[1].wait()
    hidden = w_gate.shape[0]
    gate, upper = jnp.zeros((n, hidden), F32), jnp.zeros((n, hidden), F32)
    to = iota((lines, lines), 0)
    sort = (iota((lines, lines), 1) == lax.rem(to, n) * pieces + lax.div(to, n)).astype(F32)
    sort = sort.astype(BF16)
    unsort = (iota((lines, lines), 1) == lax.rem(to, pieces) * n + lax.div(to, pieces)).astype(F32)
    unsort = unsort.astype(BF16)
    for c in range(chunks):
        settle(recv_d.at[c], inner - 1, sems[5].at[c])
        part = recv_d[c].reshape(lines, step)
        every = dot(sort, part).astype(BF16)
        for p in range(pieces):
            x = every[p * n : (p + 1) * n]
            start = p * columns + c * step
            gate += by_rows(x, w_gate[:, start : start + step])
            upper += by_rows(x, w_up[:, start : start + step])
    settle(recv_s, inner - 1, recv_sem.at[2])
    scale = recv_s[...].reshape(n, hdim)[:, :1]
    gate, upper = gate * scale, upper * scale
    inner_act = (gate * jax.nn.sigmoid(gate) * upper).astype(BF16)
    big[2].wait()
    for j in range(chunks):
        lot = []
        for p in range(pieces):
            start = p * columns + j * step
            lot.append((dot(inner_act, w_down[:, start : start + step]) * coef).astype(BF16))
        lot = dot(unsort, jnp.concatenate(lot, axis=0))
        send_e[j] = lot.astype(BF16).reshape(inner, tile, step)
        to_inner(send_e.at[j], recv_e.at[j], sems[6].at[j], sems[7].at[j], True)
        recv_e[j, b] = send_e[j, b]
    for j in range(chunks):
        settle(recv_e.at[j], inner - 1, sems[7].at[j])
        total = recv_e[j, 0].astype(F32)
        for i in range(1, inner):
            total += recv_e[j, i].astype(F32)
        send_f[j] = total.reshape(outer, pieces, step)
        to_outer(send_f.at[j], recv_f.at[j], sems[8].at[j], sems[9].at[j], True)
        recv_f[j, a] = send_f[j, a]
    for j in range(chunks):
        settle(recv_f.at[j], outer - 1, sems[9].at[j])
        mixed = (hids[j, a] + jnp.sum(recv_f[j], axis=0)).astype(BF16)
        for p in range(pieces):
            start = p * columns + j * step
            out[:, start : start + step] = mixed[p : p + 1, :]

    settle(recv1, n - 1, send_sem.at[0])
    settle(recv_r, outer - 1, send_sem.at[1])
    settle(recv_s, inner - 1, send_sem.at[2])
    for j in range(chunks):
        settle(send_a.at[j], inner - 1, sems[0].at[j])
        settle(recv_b.at[j], outer - 1, sems[2].at[j])
        settle(recv_d.at[j], inner - 1, sems[4].at[j])
        settle(send_e.at[j], inner - 1, sems[6].at[j])
        settle(send_f.at[j], outer - 1, sems[8].at[j])


def shards(
    resid, query, key, value, state, decay, out_gate, norm_gain, w_out, moe_gain,
    w_gate, w_up, w_down, expert_ids, expert_weights, *, slab_split,
):
    n = lax.axis_size("wide")
    width = resid.shape[1]
    heads, hdim = state.shape[1], state.shape[2]
    inner, outer, pieces, columns, chunks = layout(n, width)
    step = columns // chunks
    tile = outer * pieces
    hidden = w_gate.shape[1]
    hbm = pl.BlockSpec(memory_space=pltpu.HBM)
    small = (
        resid, query, key, value, decay.reshape(1, -1), out_gate, norm_gain.reshape(1, -1),
        moe_gain.reshape(1, -1), expert_ids.T, expert_weights.T,
    )
    sems = pltpu.SemaphoreType.DMA
    return pl.pallas_call(
        functools.partial(kernel, n, slab_split),
        out_shape=pltpu.VMEM(resid.shape, resid.dtype),
        in_specs=[hbm] * 15,
        out_specs=pl.BlockSpec(memory_space=pltpu.VMEM),
        scratch_shapes=[pltpu.VMEM(x.shape, x.dtype) for x in small] + [
            pltpu.VMEM((heads * hdim, hdim), F32),
            pltpu.VMEM((hdim, width), BF16),
            pltpu.VMEM((hidden, width), BF16),
            pltpu.VMEM((hidden, width), BF16),
            pltpu.VMEM((hidden, width), BF16),
            pltpu.VMEM((5, heads, hdim), F32),
            pltpu.VMEM((tile, columns), F32),
            pltpu.VMEM((chunks, outer, pieces, step), F32),
            pltpu.VMEM((heads, 1, hdim), F32),
            pltpu.VMEM((n, 1, hdim), F32),
            pltpu.VMEM((chunks, inner, tile, step), BF16),
            pltpu.VMEM((chunks, inner, tile, step), BF16),
            pltpu.VMEM((outer, pieces, columns), F32),
            pltpu.VMEM((chunks, outer, tile, step), BF16),
            pltpu.VMEM((chunks, inner, tile, step), BF16),
            pltpu.VMEM((inner, outer, 1, hdim), F32),
            pltpu.VMEM((chunks, inner, tile, step), BF16),
            pltpu.VMEM((chunks, inner, tile, step), BF16),
            pltpu.VMEM((chunks, outer, pieces, step), F32),
            pltpu.VMEM((chunks, outer, pieces, step), F32),
            sems((10,)),
            sems((STATE_CUTS + 4,)),
            sems((3,)),
            sems((3,)),
        ] + [sems((chunks,))] * 10,
        compiler_params=pltpu.CompilerParams(
            collective_id=0, has_side_effects=True, vmem_limit_bytes=VMEM
        ),
        name="decode_layer",
    )(
        *small,
        state.reshape(heads * hdim, hdim), w_out, w_gate, w_up, w_down,
    )


SPLIT = 8


def solution(mesh):
    rows = P(("group", "wide"), None)
    return jax.shard_map(
        functools.partial(shards, slab_split=SPLIT),
        mesh=mesh,
        in_specs=(
            rows, rows, rows, rows,
            P(("group", "wide"), None, None, None),
            P(), rows, P(), P("wide", None), P(),
            P("wide", None, None), P("wide", None, None), P("wide", None, None),
            P("group", None), P("group", None),
        ),
        out_specs=rows,
        check_vma=False,
    )
```

```python
import functools

import jax
import jax.numpy as jnp
from jax import lax
from jax.experimental import pallas as pl
from jax.experimental.pallas import tpu as pltpu
from jax.sharding import PartitionSpec as P

F32, BF16 = jnp.float32, jnp.bfloat16
TILE = 16
STATE_CUTS = 4
VMEM = 63 * 1024 * 1024


def iota(shape, dim):
    return lax.broadcasted_iota(jnp.int32, shape, dim)


def dot(left, right):
    return jnp.dot(left, right, preferred_element_type=F32)


def by_rows(left, weight):
    return lax.dot_general(left, weight, (((1,), (1,)), ((), ())), preferred_element_type=F32)


def layout(n, width):
    inner = 1
    while inner * inner < n:
        inner *= 2
    outer = n // inner
    pieces = max(1, TILE // outer)
    columns = width // pieces
    chunks = max(c for c in (1, 2, 3, 4) if (columns // 128) % c == 0)
    return inner, outer, pieces, columns, chunks


def kernel(
    n, slab_split,
    resid_h, query_h, key_h, value_h, decay_h, out_gate_h, norm_gain_h, moe_gain_h, ids_h, weights_h,
    state_h, w_out_h, w_gate_h, w_up_h, w_down_h,
    out,
    resid, query, key, value, decay, out_gate, norm_gain, moe_gain, ids, weights,
    state, w_out, w_gate, w_up, w_down,
    heads5, gains, hids, att3, recv1, send_a, recv_a, recv_r, recv_b, recv_d,
    recv_s, send_e, recv_e, send_f, recv_f,
    small_sem, load_sem, send_sem, recv_sem, *sems,
):
    heads, hdim = att3.shape[0], att3.shape[2]
    width = resid.shape[1]
    inner, outer, pieces, columns, chunks = layout(n, width)
    step = columns // chunks
    share = w_out_h.shape[0]
    me = lax.axis_index("wide")
    a, b = lax.div(me, inner), lax.rem(me, inner)
    tile = outer * pieces

    barrier = pltpu.get_barrier_semaphore()

    def greet(i, carry):
        pl.semaphore_signal(
            barrier, inc=1, device_id={"wide": lax.rem(me + i, n)},
            device_id_type=pl.DeviceIdType.MESH,
        )
        return carry

    small = []
    for i, (src, dst) in enumerate((
        (query_h, query), (key_h, key), (value_h, value), (out_gate_h, out_gate),
        (norm_gain_h, norm_gain), (decay_h, decay), (resid_h, resid),
        (moe_gain_h, moe_gain), (ids_h, ids), (weights_h, weights),
    )):
        small.append(pltpu.make_async_copy(src, dst, small_sem.at[i]))
        small[-1].start()
    part = state.shape[0] // STATE_CUTS
    loads = []
    for c in range(STATE_CUTS):
        at = pl.ds(c * part, part)
        loads.append(pltpu.make_async_copy(state_h.at[at], state.at[at], load_sem.at[c]))
        loads[-1].start()
    if share == hdim:
        get_out = pltpu.make_async_copy(w_out_h, w_out, load_sem.at[STATE_CUTS])
    else:
        w_out[...] = jnp.zeros_like(w_out)
        place = pl.ds(pl.multiple_of((me * share) % hdim, share), share)
        get_out = pltpu.make_async_copy(w_out_h, w_out.at[place], load_sem.at[STATE_CUTS])
    get_out.start()
    lax.fori_loop(1, n, greet, 0)

    for copy in small[:6]:
        copy.wait()
    for i, ref in enumerate((query, key, value, out_gate, norm_gain)):
        line = ref[...].astype(F32)
        for h in range(heads):
            heads5[i, h : h + 1, :] = line[:, h * hdim : (h + 1) * hdim]
    q, k, v = heads5[0], heads5[1], heads5[2]
    eye = iota((heads, heads), 0) == iota((heads, heads), 1)
    fade = jnp.sum(
        jnp.where(eye, jnp.broadcast_to(jnp.exp(-decay[...]), (heads, heads)), 0.0),
        axis=1, keepdims=True,
    )
    per_cut = heads // STATE_CUTS
    row = iota((per_cut, hdim), 0)
    cuts = []
    for c in range(STATE_CUTS):
        q_c = q[c * per_cut : (c + 1) * per_cut]
        diagonal = jnp.concatenate(
            [jnp.where(row == h, q_c, 0.0) for h in range(per_cut)], axis=1
        ).astype(BF16)
        loads[c].wait()
        cuts.append(dot(diagonal, state[pl.ds(c * part, part), :].astype(BF16)))
    att = jnp.concatenate(cuts, axis=0)
    att = fade * att + jnp.sum(q * k, axis=1, keepdims=True) * v
    mean = jnp.sum(jnp.sum(att * att, axis=1, keepdims=True), axis=0, keepdims=True) / (
        heads * hdim
    )
    attn = att * lax.rsqrt(mean + 1e-06) * heads5[4] * jax.nn.sigmoid(heads5[3])
    att3[...] = attn.reshape(heads, 1, hdim)

    pl.semaphore_wait(barrier, n - 1)

    slot = b * outer + a

    def head(device):
        return device if share == hdim else lax.div(device * share, hdim)

    for i in range(1, n):
        peer = lax.rem(me + i, n)
        pltpu.make_async_remote_copy(
            src_ref=att3.at[head(peer)], dst_ref=recv1.at[slot],
            send_sem=send_sem.at[0], recv_sem=recv_sem.at[0],
            device_id={"wide": peer}, device_id_type=pl.DeviceIdType.MESH,
        ).start()
    recv1[slot] = att3[head(me)]

    big = []
    for i, (src, dst) in enumerate(((w_gate_h, w_gate), (w_up_h, w_up), (w_down_h, w_down))):
        big.append(pltpu.make_async_copy(src.at[0], dst, load_sem.at[STATE_CUTS + 1 + i]))
        big[-1].start()

    def settle(ref, count, sem):
        view = ref.at[pl.ds(0, count)]
        pltpu.make_async_copy(view, view, sem).wait()

    def to_inner(src, dst, ssem, rsem, pick):
        for i in range(1, inner):
            peer = lax.rem(b + i, inner)
            pltpu.make_async_remote_copy(
                src_ref=src.at[peer if pick else b], dst_ref=dst.at[b],
                send_sem=ssem, recv_sem=rsem,
                device_id={"wide": a * inner + peer}, device_id_type=pl.DeviceIdType.MESH,
            ).start()

    def to_outer(src, dst, ssem, rsem, pick):
        for i in range(1, outer):
            peer = lax.rem(a + i, outer)
            pltpu.make_async_remote_copy(
                src_ref=src.at[peer if pick else a], dst_ref=dst.at[a],
                send_sem=ssem, recv_sem=rsem,
                device_id={"wide": peer * inner + b}, device_id_type=pl.DeviceIdType.MESH,
            ).start()

    for copy in small[6:]:
        copy.wait()

    lines = n * pieces
    to = iota((lines, lines), 0)
    sort = (iota((lines, lines), 1) == lax.rem(to, n) * pieces + lax.div(to, n)).astype(F32)
    sort = sort.astype(BF16)
    unsort = (iota((lines, lines), 1) == lax.rem(to, pieces) * n + lax.div(to, pieces)).astype(F32)
    unsort = unsort.astype(BF16)

    owner = me // slab_split
    coef = jnp.sum(jnp.where(ids[...] == owner, weights[...], 0.0), axis=0, keepdims=True)
    line = iota((n, n), 0)
    request = lax.rem(line, outer) * inner + lax.div(line, outer)
    coef = jnp.sum(
        jnp.where(request == iota((n, n), 1), jnp.broadcast_to(coef, (n, n)), 0.0),
        axis=1, keepdims=True,
    )

    line = resid[...].astype(F32)
    for p in range(pieces):
        recv_r[a, p : p + 1, :] = line[:, p * columns : (p + 1) * columns]
        for i in range(outer):
            at = i * pieces + p
            gains[at : at + 1, :] = moe_gain[:, p * columns : (p + 1) * columns]
    to_outer(recv_r, recv_r, send_sem.at[1], recv_sem.at[1], False)

    get_out.wait()
    settle(recv1, n - 1, recv_sem.at[0])
    features = recv1[...].reshape(n, hdim).astype(BF16)
    for c in range(chunks):
        lot = []
        for p in range(pieces):
            start = p * columns + c * step
            lot.append(dot(features, w_out[:, start : start + step]).astype(BF16))
        lot = dot(unsort, jnp.concatenate(lot, axis=0))
        send_a[c] = lot.astype(BF16).reshape(inner, tile, step)
        to_inner(send_a.at[c], recv_a.at[c], sems[0].at[c], sems[1].at[c], True)
        recv_a[c, b] = send_a[c, b]
    for c in range(chunks):
        settle(recv_a.at[c], inner - 1, sems[1].at[c])
        total = recv_a[c, 0].astype(F32)
        for i in range(1, inner):
            total += recv_a[c, i].astype(F32)
        recv_b[c, a] = total.astype(BF16)
        to_outer(recv_b.at[c], recv_b.at[c], sems[2].at[c], sems[3].at[c], False)
    settle(recv_r, outer - 1, recv_sem.at[1])
    squares = jnp.zeros((tile, 1), F32)
    for c in range(chunks):
        settle(recv_b.at[c], outer - 1, sems[3].at[c])
        total = recv_b[c, 0].astype(F32)
        for i in range(1, outer):
            total += recv_b[c, i].astype(F32)
        at = slice(c * step, (c + 1) * step)
        hid = (recv_r[:, :, at].reshape(tile, step) + total).astype(BF16).astype(F32)
        recv_d[c, b] = (hid * gains[:, at]).astype(BF16)
        to_inner(recv_d.at[c], recv_d.at[c], sems[4].at[c], sems[5].at[c], False)
        hids[c] = hid.reshape(outer, pieces, step)
        squares += jnp.sum(hid * hid, axis=1, keepdims=True)
    mates = iota((tile, outer), 0) // pieces == iota((tile, outer), 1)
    mean = jnp.sum(
        jnp.where(mates, jnp.broadcast_to(squares, (tile, outer)), 0.0), axis=0, keepdims=True
    ) / width
    same = iota((outer, outer), 0) == iota((outer, outer), 1)
    scale = jnp.sum(
        jnp.where(same, jnp.broadcast_to(lax.rsqrt(mean + 1e-06), (outer, outer)), 0.0),
        axis=1, keepdims=True,
    )
    recv_s[b] = jnp.broadcast_to(scale, (outer, hdim)).reshape(outer, 1, hdim)
    to_inner(recv_s, recv_s, send_sem.at[2], recv_sem.at[2], False)

    big[0].wait()
    big[1].wait()
    hidden = w_gate.shape[0]
    gate, upper = jnp.zeros((n, hidden), F32), jnp.zeros((n, hidden), F32)
    for c in range(chunks):
        settle(recv_d.at[c], inner - 1, sems[5].at[c])
        part = recv_d[c].reshape(lines, step)
        every = dot(sort, part).astype(BF16)
        for p in range(pieces):
            x = every[p * n : (p + 1) * n]
            start = p * columns + c * step
            gate += by_rows(x, w_gate[:, start : start + step])
            upper += by_rows(x, w_up[:, start : start + step])
    settle(recv_s, inner - 1, recv_sem.at[2])
    scale = recv_s[...].reshape(n, hdim)[:, :1]
    gate, upper = gate * scale, upper * scale
    inner_act = (gate * jax.nn.sigmoid(gate) * upper).astype(BF16)
    big[2].wait()
    for j in range(chunks):
        lot = []
        for p in range(pieces):
            start = p * columns + j * step
            lot.append((dot(inner_act, w_down[:, start : start + step]) * coef).astype(BF16))
        lot = dot(unsort, jnp.concatenate(lot, axis=0))
        send_e[j] = lot.astype(BF16).reshape(inner, tile, step)
        to_inner(send_e.at[j], recv_e.at[j], sems[6].at[j], sems[7].at[j], True)
        recv_e[j, b] = send_e[j, b]
    for j in range(chunks):
        settle(recv_e.at[j], inner - 1, sems[7].at[j])
        total = recv_e[j, 0].astype(F32)
        for i in range(1, inner):
            total += recv_e[j, i].astype(F32)
        send_f[j] = total.reshape(outer, pieces, step)
        to_outer(send_f.at[j], recv_f.at[j], sems[8].at[j], sems[9].at[j], True)
        recv_f[j, a] = send_f[j, a]
    for j in range(chunks):
        settle(recv_f.at[j], outer - 1, sems[9].at[j])
        mixed = (hids[j, a] + jnp.sum(recv_f[j], axis=0)).astype(BF16)
        for p in range(pieces):
            start = p * columns + j * step
            out[:, start : start + step] = mixed[p : p + 1, :]

    settle(recv1, n - 1, send_sem.at[0])
    settle(recv_r, outer - 1, send_sem.at[1])
    settle(recv_s, inner - 1, send_sem.at[2])
    for j in range(chunks):
        settle(send_a.at[j], inner - 1, sems[0].at[j])
        settle(recv_b.at[j], outer - 1, sems[2].at[j])
        settle(recv_d.at[j], inner - 1, sems[4].at[j])
        settle(send_e.at[j], inner - 1, sems[6].at[j])
        settle(send_f.at[j], outer - 1, sems[8].at[j])


def shards(
    resid, query, key, value, state, decay, out_gate, norm_gain, w_out, moe_gain,
    w_gate, w_up, w_down, expert_ids, expert_weights, *, slab_split,
):
    n = lax.axis_size("wide")
    width = resid.shape[1]
    heads, hdim = state.shape[1], state.shape[2]
    inner, outer, pieces, columns, chunks = layout(n, width)
    step = columns // chunks
    tile = outer * pieces
    hidden = w_gate.shape[1]
    hbm = pl.BlockSpec(memory_space=pltpu.HBM)
    small = (
        resid, query, key, value, decay.reshape(1, -1), out_gate, norm_gain.reshape(1, -1),
        moe_gain.reshape(1, -1), expert_ids.T, expert_weights.T,
    )
    sems = pltpu.SemaphoreType.DMA
    return pl.pallas_call(
        functools.partial(kernel, n, slab_split),
        out_shape=pltpu.VMEM(resid.shape, resid.dtype),
        in_specs=[hbm] * 15,
        out_specs=pl.BlockSpec(memory_space=pltpu.VMEM),
        scratch_shapes=[pltpu.VMEM(x.shape, x.dtype) for x in small] + [
            pltpu.VMEM((heads * hdim, hdim), F32),
            pltpu.VMEM((hdim, width), BF16),
            pltpu.VMEM((hidden, width), BF16),
            pltpu.VMEM((hidden, width), BF16),
            pltpu.VMEM((hidden, width), BF16),
            pltpu.VMEM((5, heads, hdim), F32),
            pltpu.VMEM((tile, columns), F32),
            pltpu.VMEM((chunks, outer, pieces, step), F32),
            pltpu.VMEM((heads, 1, hdim), F32),
            pltpu.VMEM((n, 1, hdim), F32),
            pltpu.VMEM((chunks, inner, tile, step), BF16),
            pltpu.VMEM((chunks, inner, tile, step), BF16),
            pltpu.VMEM((outer, pieces, columns), F32),
            pltpu.VMEM((chunks, outer, tile, step), BF16),
            pltpu.VMEM((chunks, inner, tile, step), BF16),
            pltpu.VMEM((inner, outer, 1, hdim), F32),
            pltpu.VMEM((chunks, inner, tile, step), BF16),
            pltpu.VMEM((chunks, inner, tile, step), BF16),
            pltpu.VMEM((chunks, outer, pieces, step), F32),
            pltpu.VMEM((chunks, outer, pieces, step), F32),
            sems((10,)),
            sems((STATE_CUTS + 4,)),
            sems((3,)),
            sems((3,)),
        ] + [sems((chunks,))] * 10,
        compiler_params=pltpu.CompilerParams(
            collective_id=0, has_side_effects=True, vmem_limit_bytes=VMEM
        ),
        name="decode_layer",
    )(
        *small,
        state.reshape(heads * hdim, hdim), w_out, w_gate, w_up, w_down,
    )


SPLIT = 8


def solution(mesh):
    rows = P(("group", "wide"), None)
    return jax.shard_map(
        functools.partial(shards, slab_split=SPLIT),
        mesh=mesh,
        in_specs=(
            rows, rows, rows, rows,
            P(("group", "wide"), None, None, None),
            P(), rows, P(), P("wide", None), P(),
            P("wide", None, None), P("wide", None, None), P("wide", None, None),
            P("group", None), P("group", None),
        ),
        out_specs=rows,
        check_vma=False,
    )
```
